32 devices in a mesh: groups: 2 (over y), row: 4 (over z), col: 4 (over x, core).
Axes of the slice: x: 2, y: 2, z: 4, core: 2. Of those that a mesh axis runs over, the one named last changes fastest.
Arguments:
- xval: bfloat16 [192, 12, 128, 128], P(('groups', 'row', 'col')), parts along dimension 0, may hold values from -5 to 5
- cols: int32 [192, 12], P(('groups', 'row', 'col')), parts along dimension 0, may hold values from 0 to 95, as said below
- keep: int32 [192, 12], P(('groups', 'row', 'col')), parts along dimension 0, may hold values 0 or 1
- flag: int32 [2], P('groups'), parts along dimension 0, may hold values from 0 to 1
Outputs:
- purified: bfloat16 [192, 12, 128, 128], P(('groups', 'row', 'col')), parts along dimension 0
- occupation: float32 [2], P('groups'), parts along dimension 0
The draws below stay inside these ranges and needn't reach their ends.
There are 2 independent parts, one for each index of `groups`. The reference program is written for one: setup_inputs(seed, part) draws one part's arguments, and reference() takes and returns one part's arrays. A program takes and returns all parts, laid end to end along the dimension named above; each array names one. Nothing has to cross between parts.
Inputs may be any that keep to these rules, and one draw needn't show every extreme that they name: cols[i, 0] = i. The entries of one list are distinct. Device d in the order row+col holds block rows d * 6 to d * 6 + 5. Every list names all 6 rows of its own device; its other entries lie in the rows of the 1 device on either side of it in that order, wrapping at the ends, and the lists of one device name exactly 4 distinct rows of each of those 2 devices.
All inputs are finite; a program needn't handle non-finite values. No bound on the sum of `keep` on one device may be relied on, other than what follows from the above.
Results may differ from the reference program's by a relative error of at most 0.001.
Values may be sent and summed in bfloat16 or wider, within the bound.
No kernel may reach another device: no remote copies, remote signals or barrier semaphores. Data moves between devices by JAX's collectives and lax.ppermute only.
A program may use at most 128 MiB of HBM per device.

```python
import jax
import jax.numpy as jnp
from jax import lax

B = 128
RB = 6
K = 12
PEERS = 1
CAP = 4
NBR = 96


def draw_cols(key, part):
    key = jax.random.fold_in(key, 11)
    device_count = NBR // RB
    reach_count = 2 * PEERS * CAP
    spare_count = reach_count - (K - RB)
    stride = max(1, reach_count // RB)
    peer_keys = jax.random.split(jax.random.fold_in(key, 1), device_count * 2 * PEERS)
    peer_perms = jax.vmap(lambda one_key: jax.random.permutation(one_key, RB))(peer_keys)
    picked = peer_perms[:, :CAP].reshape(device_count, 2 * PEERS, CAP).astype(jnp.int32)
    offset_list = jnp.array(list(range(1, PEERS + 1)) + list(range(-PEERS, 0)), dtype=jnp.int32)
    device_ids = jnp.arange(device_count, dtype=jnp.int32)
    peer_devices = (device_ids[:, None] + offset_list[None, :]) % device_count
    candidates = (peer_devices[:, :, None] * RB + picked).reshape(device_count, reach_count)
    order_keys = jax.random.split(jax.random.fold_in(key, 2), device_count)
    orders = jax.vmap(lambda one_key: jax.random.permutation(one_key, reach_count))(order_keys)
    shuffled = jnp.take_along_axis(candidates, orders.astype(jnp.int32), axis=1)
    local_ids = jnp.arange(RB, dtype=jnp.int32)
    kept_places = (local_ids[:, None] * stride + spare_count + jnp.arange(K - RB, dtype=jnp.int32)[None, :]) % reach_count
    far_cols = shuffled[:, kept_places]
    own_base = device_ids[:, None, None] * RB
    self_cols = own_base + local_ids[None, :, None]
    others = (local_ids[:, None] + 1 + jnp.arange(RB - 1, dtype=jnp.int32)[None, :]) % RB
    other_cols = own_base + others[None, :, :]
    tail_cols = jnp.concatenate([other_cols, far_cols], axis=2).reshape(NBR, K - 1)
    mix_keys = jax.random.split(jax.random.fold_in(key, 3), NBR)
    mixings = jax.vmap(lambda one_key: jax.random.permutation(one_key, K - 1))(mix_keys)
    tail_cols = jnp.take_along_axis(tail_cols, mixings.astype(jnp.int32), axis=1)
    head_cols = self_cols.reshape(NBR, 1)
    return jnp.concatenate([head_cols, tail_cols], axis=1).astype(jnp.int32)


def draw_xval(key, part):
    key = jax.random.fold_in(key, 23)
    noise_key = jax.random.fold_in(key, 1)
    scale_key = jax.random.fold_in(key, 2)
    lift_key = jax.random.fold_in(key, 3)
    ramp = jnp.arange(NBR, dtype=jnp.float32) / (NBR - 1)
    noise = jnp.clip(jax.random.normal(noise_key, (NBR, K, B, B), jnp.float32), -6.0, 6.0)
    row_scale = jnp.exp(jax.random.uniform(scale_key, (NBR,), jnp.float32, jnp.log(0.5), jnp.log(2.0)))
    diag_lift = (0.15 + 0.75 * ramp) * jax.random.uniform(lift_key, (NBR,), jnp.float32, 0.9, 1.1)
    blocks = 0.2 * row_scale[:, None, None, None] * noise
    identity = jnp.eye(B, dtype=jnp.float32)
    blocks = blocks.at[:, 0].add(diag_lift[:, None, None] * identity[None, :, :])
    return blocks.astype(jnp.bfloat16)


def set_ends(drawn, own_key, low, high):
    place = [jax.random.randint(jax.random.fold_in(own_key, axis), (), 0, length) for axis, length in enumerate(drawn.shape)]
    longest = drawn.shape.index(max(drawn.shape))
    beside = place[:longest] + [(place[longest] + 1) % drawn.shape[longest]] + place[longest + 1:]
    return drawn.at[tuple(place)].set(low).at[tuple(beside)].set(high)


def setup_inputs(seed: int = 0, part: int = 0) -> dict:
    arg_keys = jax.random.split(jax.random.key(seed), 5)
    part_keys = jax.random.split(jax.random.fold_in(arg_keys[4], part), 5)
    xval = draw_xval(jax.random.fold_in(jax.random.fold_in(arg_keys[4], part), 71), part)
    cols = draw_cols(jax.random.fold_in(jax.random.fold_in(arg_keys[4], part), 71), part)
    keep = set_ends((jax.random.randint(part_keys[2], (NBR, K), 0, 4) < 3).astype(jnp.int32), jax.random.fold_in(part_keys[2], 1), 0, 1)
    flag = jax.random.randint(part_keys[3], (1,), 0, 2).astype(jnp.int32)
    return {"xval": xval, "cols": cols, "keep": keep, "flag": flag}


def reference(xval, cols, keep, flag):
    def square_row(row_index):
        left_blocks = xval[row_index].astype(jnp.float32)
        neighbors = cols[row_index]
        right_blocks = jnp.take(xval, neighbors, axis=0).astype(jnp.float32)
        right_cols = jnp.take(cols, neighbors, axis=0)
        products = jnp.einsum('tab,tubc->tuac', left_blocks, right_blocks, precision=lax.Precision.HIGHEST)
        selector = (right_cols[:, None, :] == neighbors[None, :, None]).astype(jnp.float32)
        return jnp.einsum('tsu,tuac->sac', selector, products, precision=lax.Precision.HIGHEST)

    square = lax.map(square_row, jnp.arange(NBR, dtype=jnp.int32))
    kept_mask = keep[:, :, None, None].astype(jnp.float32)
    square = square * kept_mask
    fresh_values = jnp.where(flag[0] == 1, square, 2.0 * xval.astype(jnp.float32) * kept_mask - square)
    occupation = jnp.sum(jnp.trace(fresh_values[:, 0], axis1=1, axis2=2)) / (NBR * B)
    return fresh_values.astype(jnp.bfloat16), jnp.reshape(occupation, (1,)).astype(jnp.float32)
```

```python
import jax
import jax.numpy as jnp
from jax import lax
from jax.experimental import pallas as pl
from jax.experimental.pallas import tpu as pltpu
from jax.sharding import PartitionSpec as P

CAP = 4
RING = ("row", "col")
SMEM = pl.BlockSpec(memory_space=pltpu.SMEM)
VMEM = pl.BlockSpec(memory_space=pltpu.VMEM)
ANY = pl.BlockSpec(memory_space=pl.ANY)


def shift(block, distance):
    n = lax.axis_size(RING)
    return lax.ppermute(block, RING, [(i, (i + distance) % n) for i in range(n)])


def ring_sum(value):
    n = lax.axis_size(RING)
    if n & (n - 1):
        return lax.psum(value, RING)
    step = 1
    while step < n:
        value = value + lax.ppermute(value, RING, [(i, i ^ step) for i in range(n)])
        step *= 2
    return value


def scan_own(cols, table, names, total_rows):
    rows, slots = cols.shape
    wide = 3 * rows
    base = cols[0, 0]
    for q in range(rows * wide):
        table[q] = -1
    for q in range(wide):
        names[q] = 0
    for i in range(rows):
        for s in range(slots):
            rel = cols[i, s] - base
            rel = jnp.where(rel < 0, rel + total_rows, rel)
            rel = jnp.where(rel >= 2 * rows, rel - (total_rows - wide), rel)
            table[i * wide + rel] = s
            names[rel] = 1


def scan_peer(cols, names, base):
    rows, slots = cols.shape
    for q in range(rows + 1):
        names[q] = 0
    for i in range(rows):
        for s in range(slots):
            rel = cols[i, s] - base
            inside = (rel >= 0) & (rel < rows)
            names[jnp.where(inside, rel, rows)] = 1


def rank(names, start, rows, order):
    count = 0
    for r in range(rows):
        named = names[start + r]
        order[jnp.where(named > 0, jnp.minimum(count, CAP), CAP)] = r
        count = count + named


def put_block(x, zeros, table, row, column, wide, target, a, b, sem):
    block = x.shape[-1]
    slot = table[row * wide + column]
    place = target.at[pl.ds(a * block, block), pl.ds(b * block, block)]

    @pl.when(slot >= 0)
    def _():
        pltpu.make_async_copy(x.at[row, slot], place, sem).start()

    @pl.when(slot < 0)
    def _():
        pltpu.make_async_copy(zeros, place, sem).start()


def pack_ahead(total_rows, cols, x, far, zeros, table, names, order, sem):
    rows = cols.shape[0]
    wide = 3 * rows
    zeros[...] = jnp.zeros_like(zeros)
    scan_own(cols, table, names, total_rows)
    rank(names, rows, rows, order)
    for i in range(rows):
        for c in range(CAP):
            put_block(x, zeros, table, i, rows + order[c], wide, far, i, c, sem)
    pltpu.make_async_copy(far, far, sem).wait()


def pack_named(total_rows, cols, cols_ahead, cols_behind, x, near_ahead, far_behind, near_behind,
               zeros, table, names, order, peer, asked_ahead, asked_behind, sem):
    rows = cols.shape[0]
    wide = 3 * rows
    zeros[...] = jnp.zeros_like(zeros)
    scan_own(cols, table, names, total_rows)
    rank(names, 2 * rows, rows, order)
    base = cols[0, 0]
    scan_peer(cols_ahead, peer, base)
    rank(peer, 0, rows, asked_ahead)
    scan_peer(cols_behind, peer, base)
    rank(peer, 0, rows, asked_behind)
    for a in range(CAP):
        for b in range(CAP):
            put_block(x, zeros, table, asked_ahead[a], asked_ahead[b], wide, near_ahead, a, b, sem.at[0])
            put_block(x, zeros, table, asked_behind[a], 2 * rows + order[b], wide, far_behind, a, b, sem.at[1])
            put_block(x, zeros, table, asked_behind[a], asked_behind[b], wide, near_behind, a, b, sem.at[2])
    for k, out in enumerate((near_ahead, far_behind, near_behind)):
        pltpu.make_async_copy(out, out, sem.at[k]).wait()


def eye_sum(blocks):
    n = blocks.shape[-1]
    on = lax.broadcasted_iota(jnp.int32, (n, n), 0) == lax.broadcasted_iota(jnp.int32, (n, n), 1)
    return jnp.where(on, blocks, 0.0)


def own_part(total_rows, cols, keep, flag, x, lo, lp, lm, so, sp, sm, trace, table, names, order_p, order_m):
    rows = cols.shape[0]
    wide = 3 * rows
    block = x.shape[-1]
    scan_own(cols, table, names, total_rows)
    rank(names, rows, rows, order_p)
    rank(names, 2 * rows, rows, order_m)
    for i in range(rows):
        span = pl.ds(i * block, block)
        for k in range(rows):
            lo[span, pl.ds(k * block, block)] = x[i, table[i * wide + k]]
        for c in range(CAP):
            for out, start, order in ((lp, rows, order_p), (lm, 2 * rows, order_m)):
                slot = table[i * wide + start + order[c]]
                value = x[i, jnp.maximum(slot, 0)]
                out[span, pl.ds(c * block, block)] = jnp.where(slot >= 0, value, jnp.zeros_like(value))
    left = lo[...]
    so[...] = jnp.dot(left, left, preferred_element_type=jnp.float32)
    sp[...] = jnp.dot(left, lp[...], preferred_element_type=jnp.float32)
    sm[...] = jnp.dot(left, lm[...], preferred_element_type=jnp.float32)
    twice = jnp.where(flag[0] == 1, 0.0, 2.0)
    sign = jnp.where(flag[0] == 1, 1.0, -1.0)
    total = jnp.zeros((block, block), jnp.float32)
    for i in range(rows):
        span = pl.ds(i * block, block)
        kept = keep[i, 0].astype(jnp.float32)
        total = total + (kept * twice) * lo[span, span].astype(jnp.float32) + (kept * sign) * so[span, span]
    trace[...] = jnp.sum(eye_sum(total), axis=0, keepdims=True)


def trace_part(total_rows, cols, keep, flag, cols_behind, keep_behind, lm, far, trace_own, trace, table, names, order, peer, asked):
    rows = cols.shape[0]
    block = lm.shape[0] // rows
    scan_own(cols, table, names, total_rows)
    rank(names, 2 * rows, rows, order)
    scan_peer(cols_behind, peer, cols[0, 0])
    rank(peer, 0, rows, asked)
    sign = jnp.where(flag[0] == 1, 1.0, -1.0)
    total = jnp.zeros((block, block), jnp.float32)
    for r in range(CAP):
        theirs = order[r]
        for c in range(CAP):
            mine = asked[c]
            weight = sign * (keep[mine, 0] + keep_behind[theirs, 0]).astype(jnp.float32)
            left = far[pl.ds(pl.multiple_of(theirs * block, block), block), pl.ds(c * block, block)]
            right = lm[pl.ds(pl.multiple_of(mine * block, block), block), pl.ds(r * block, block)]
            total = total + weight * jnp.dot(left, right, preferred_element_type=jnp.float32)
    trace[...] = trace_own[...] + jnp.sum(eye_sum(total), axis=0, keepdims=True)


def finish(keep, flag, i, slot, value, square):
    kept = keep[i, slot].astype(jnp.float32)
    twice = kept * jnp.where(flag[0] == 1, 0.0, 2.0)
    sign = kept * jnp.where(flag[0] == 1, 1.0, -1.0)
    return (twice * value.astype(jnp.float32) + sign * square).astype(jnp.bfloat16)


def middle_part(total_rows, cols, keep, flag, cols_ahead, cols_behind, lo, lp, lm, so, sm, far, near_m, far_p, out,
                own, behind, stage, table, names, order_m, peer, asked_p, asked_m, sem):
    rows = cols.shape[0]
    wide = 3 * rows
    block = lo.shape[0] // rows
    scan_own(cols, table, names, total_rows)
    rank(names, 2 * rows, rows, order_m)
    scan_peer(cols_ahead, peer, cols[0, 0])
    rank(peer, 0, rows, asked_p)
    scan_peer(cols_behind, peer, cols[0, 0])
    rank(peer, 0, rows, asked_m)
    own[...] = so[...]
    picked = jnp.concatenate(
        [far[pl.ds(pl.multiple_of(order_m[r] * block, block), block), :] for r in range(CAP)], axis=0)
    for left, right, asked in ((lm, picked, asked_m), (lp, far_p[...], asked_p)):
        part = jnp.dot(left[...], right, preferred_element_type=jnp.float32)
        for c in range(CAP):
            place = pl.ds(pl.multiple_of(asked[c] * block, block), block)
            own[:, place] = own[:, place] + part[:, c * block:(c + 1) * block]
    behind[...] = sm[...] + jnp.dot(lm[...], near_m[...], preferred_element_type=jnp.float32)
    for i in range(rows):
        span = pl.ds(i * block, block)
        for k in range(rows):
            slot = table[i * wide + k]
            col = pl.ds(k * block, block)
            stage[i, k] = finish(keep, flag, i, slot, lo[span, col], own[span, col])
            pltpu.make_async_copy(stage.at[i, k], out.at[i, slot], sem).start()
        for c in range(CAP):
            slot = table[i * wide + 2 * rows + order_m[c]]
            col = pl.ds(c * block, block)
            stage[i, rows + c] = finish(keep, flag, i, jnp.maximum(slot, 0), lm[span, col], behind[span, col])

            @pl.when(slot >= 0)
            def _():
                pltpu.make_async_copy(stage.at[i, rows + c], out.at[i, slot], sem).start()
    for i in range(rows):
        for k in range(rows):
            pltpu.make_async_copy(stage.at[i, k], out.at[i, 0], sem).wait()
        for c in range(CAP):
            slot = table[i * wide + 2 * rows + order_m[c]]

            @pl.when(slot >= 0)
            def _():
                pltpu.make_async_copy(stage.at[i, rows + c], out.at[i, slot], sem).wait()


def last_part(total_rows, cols, keep, flag, lp, sp, near_p, _, out, stage, table, names, order_p, sem):
    rows = cols.shape[0]
    wide = 3 * rows
    block = lp.shape[0] // rows
    scan_own(cols, table, names, total_rows)
    rank(names, rows, rows, order_p)
    for i in range(rows):
        span = pl.ds(i * block, block)
        square = sp[span, :] + jnp.dot(lp[span, :], near_p[...], preferred_element_type=jnp.float32)
        for c in range(CAP):
            slot = table[i * wide + rows + order_p[c]]
            col = pl.ds(c * block, block)
            stage[i, c] = finish(keep, flag, i, jnp.maximum(slot, 0), lp[span, col], square[:, c * block:(c + 1) * block])

            @pl.when(slot >= 0)
            def _():
                pltpu.make_async_copy(stage.at[i, c], out.at[i, slot], sem).start()
    for i in range(rows):
        for c in range(CAP):
            slot = table[i * wide + rows + order_p[c]]

            @pl.when(slot >= 0)
            def _():
                pltpu.make_async_copy(stage.at[i, c], out.at[i, slot], sem).wait()


def body(x, cols, keep, flag):
    rows, slots, block = x.shape[0], x.shape[1], x.shape[2]
    total_rows = rows * lax.axis_size(RING)
    table = pltpu.SMEM((rows * 3 * rows,), jnp.int32)
    names = pltpu.SMEM((3 * rows,), jnp.int32)
    peer = pltpu.SMEM((rows + 1,), jnp.int32)
    order = pltpu.SMEM((CAP + 1,), jnp.int32)
    zeros = pltpu.VMEM((block, block), x.dtype)
    bf16, f32 = jnp.bfloat16, jnp.float32
    wide, narrow = rows * block, CAP * block

    def call(kernel, shapes, out_specs, in_specs, scratch, name, aliases=None):
        def named(*refs):
            kernel(total_rows, *refs)
        return pl.pallas_call(
            named, out_shape=[jax.ShapeDtypeStruct(*s) for s in shapes], in_specs=in_specs, out_specs=out_specs,
            scratch_shapes=scratch, name=name, input_output_aliases=aliases or {},
            compiler_params=pltpu.CompilerParams(vmem_limit_bytes=48 * 1024 * 1024))

    both = jnp.concatenate([cols, keep], axis=0)
    from_behind = shift(both, 1)
    cols_ahead = shift(cols, -1)
    cols_behind, keep_behind = from_behind[:rows], from_behind[rows:]
    far_send, = call(pack_ahead, [((wide, narrow), bf16)], [ANY], [SMEM, ANY],
                     [zeros, table, names, order, pltpu.SemaphoreType.DMA], "pack_ahead")(cols, x)
    far = shift(far_send, 1)
    near_ahead, far_behind, near_behind = call(
        pack_named, [((narrow, narrow), bf16)] * 3, [ANY] * 3, [SMEM] * 3 + [ANY],
        [zeros, table, names, order, peer, order, order, pltpu.SemaphoreType.DMA((3,))], "pack_named",
    )(cols, cols_ahead, cols_behind, x)
    near_m = shift(near_ahead, 1)
    far_p = shift(far_behind, -1)
    near_p = shift(near_behind, -1)
    lo, lp, lm, so, sp, sm, trace = call(
        own_part,
        [((wide, wide), bf16), ((wide, narrow), bf16), ((wide, narrow), bf16),
         ((wide, wide), f32), ((wide, narrow), f32), ((wide, narrow), f32), ((1, block), f32)],
        [VMEM] * 7, [SMEM] * 3 + [VMEM], [table, names, order, order], "own_part")(cols, keep, flag, x)
    trace, = call(trace_part, [((1, block), f32)], [VMEM], [SMEM] * 5 + [VMEM] * 3,
                  [table, names, order, peer, order], "trace_part",
                  )(cols, keep, flag, cols_behind, keep_behind, lm, far, trace)
    partial = jnp.sum(trace).reshape(1) * (1.0 / (total_rows * block))
    occupation = ring_sum(partial)
    out, = call(
        middle_part, [(x.shape, bf16)], [ANY], [SMEM] * 5 + [VMEM] * 8,
        [pltpu.VMEM((wide, wide), f32), pltpu.VMEM((wide, narrow), f32),
         pltpu.VMEM((rows, rows + CAP, block, block), bf16), table, names, order, peer, order, order,
         pltpu.SemaphoreType.DMA],
        "middle_part")(cols, keep, flag, cols_ahead, cols_behind, lo, lp, lm, so, sm, far, near_m, far_p)
    out, = call(
        last_part, [(x.shape, bf16)], [ANY], [SMEM] * 3 + [VMEM] * 3 + [ANY],
        [pltpu.VMEM((rows, CAP, block, block), bf16), table, names, order, pltpu.SemaphoreType.DMA],
        "last_part", {6: 0})(cols, keep, flag, lp, sp, near_p, out)
    return out, occupation


def solution(mesh):
    placed = (
        P(("groups", "row", "col"), None, None, None),
        P(("groups", "row", "col"), None),
        P(("groups", "row", "col"), None),
        P("groups"),
    )
    return jax.shard_map(
        body,
        mesh=mesh,
        in_specs=placed,
        out_specs=(P(("groups", "row", "col"), None, None, None), P("groups")),
        check_vma=False,
    )
```

```python
import functools

import jax
import jax.numpy as jnp
from jax import lax
from jax.experimental import pallas as pl
from jax.experimental.pallas import tpu as pltpu
from jax.sharding import PartitionSpec as P

CAP = 4
RING = ("row", "col")
SMEM = pl.BlockSpec(memory_space=pltpu.SMEM)
VMEM = pl.BlockSpec(memory_space=pltpu.VMEM)
HBM = pl.BlockSpec(memory_space=pltpu.HBM)
MIB = 1024 * 1024


def permute(value, pairs):
    return lax.ppermute(value, RING, pairs)


def ring_sum(value):
    n, cols = lax.axis_size(RING), lax.axis_size("col")
    if n & (n - 1) or cols & (cols - 1):
        return lax.psum(value, RING)
    steps = [1] + [cols << k for k in range((n // cols).bit_length() - 1)] + [2 << k for k in range(cols.bit_length() - 2)]
    for step in steps:
        value = value + permute(value, [(i, i ^ step) for i in range(n)])
    return value


def rank(bits, rows, order, first):
    count = 0
    for r in range(rows):
        named = lax.rem(lax.shift_right_logical(bits, r), 2)
        order[first + jnp.where(named > 0, jnp.minimum(count, CAP), CAP)] = r
        count = count + named


def clear(ref, count, value):
    for q in range(count):
        ref[q] = value


def copy_in(source, target, sem):
    copy = pltpu.make_async_copy(source, target, sem)
    copy.start()
    return copy


def spread_kernel(total_rows, cols_hbm, keep_hbm, flag, x_hbm, own, outer, inner, table, meta,
                  cols, keep, x, slots_of, order, sem):
    rows, slots = cols.shape
    block = x.shape[-1]
    wide = 3 * rows
    across = rows + 2 * CAP
    lists = [copy_in(cols_hbm, cols, sem.at[0]), copy_in(keep_hbm, keep, sem.at[1])]
    blocks = [copy_in(x_hbm.at[i], x.at[i], sem.at[2 + i]) for i in range(rows)]
    clear(slots_of, rows * wide, -1)
    for copy in lists:
        copy.wait()
    base = cols[0, 0]
    odd = lax.rem(lax.div(base, rows), 2)
    ahead = jnp.where(odd == 1, 0, rows)
    behind = jnp.where(odd == 1, 2 * rows, rows) - (total_rows - rows)
    bits = 0
    for i in range(rows):
        for s in range(slots):
            rel = cols[i, s] - base
            rel = jnp.where(rel < 0, rel + total_rows, rel)
            rel = rel + jnp.where(rel >= 2 * rows, behind, jnp.where(rel >= rows, ahead, 0))
            slots_of[i * wide + rel] = 2 * s + keep[i, s]
            bits = bits | lax.shift_left(1, rel)
    rank(lax.shift_right_logical(bits, rows), rows, order, 0)
    rank(lax.shift_right_logical(bits, 2 * rows), rows, order, CAP + 1)
    for c in range(2 * CAP):
        meta[c] = order[c + c // CAP]
    meta[2 * CAP] = base
    meta[2 * CAP + 1] = flag[0]
    for i in range(rows):
        span = pl.ds(i * block, block)
        blocks[i].wait()
        for k in range(rows):
            code = slots_of[i * wide + k]
            table[i * across + k] = code
            own[span, pl.ds(k * block, block)] = x[i, lax.shift_right_logical(code, 1)]
        for first, target, start, shift in ((0, outer, rows, 0), (CAP + 1, inner, 2 * rows, CAP)):
            for c in range(CAP):
                code = slots_of[i * wide + start + order[first + c]]
                table[i * across + rows + shift + c] = code
                value = x[i, lax.shift_right_logical(jnp.maximum(code, 0), 1)]
                target[span, pl.ds(c * block, block)] = jnp.where(code >= 0, value, jnp.zeros_like(value))


def pack_kernel(meta, cols_outer, own, outer, far_out, near_out, asked, order, stage, sem):
    rows, slots = cols_outer.shape
    block = own.shape[0] // rows
    half = CAP * block
    base = meta[2 * CAP]
    bits = 0
    for i in range(rows):
        for s in range(slots):
            rel = cols_outer[i, s] - base
            bits = bits | lax.shift_left(1, jnp.where((rel >= 0) & (rel < rows), rel, rows))
    rank(bits, rows, order, 0)
    copies = []
    for a in range(CAP):
        asked[a] = order[a]
        span = pl.ds(a * block, block)
        row = pl.ds(pl.multiple_of(order[a] * block, block), block)
        stage[span, 0:half] = outer[row, :]
        for b in range(CAP):
            column = pl.ds(pl.multiple_of(order[b] * block, block), block)
            stage[span, pl.ds(half + b * block, block)] = own[row, column]
        copies.append(copy_in(stage.at[span, 0:half], far_out.at[span, :], sem.at[0]))
        copies.append(copy_in(stage.at[span, half:2 * half], near_out.at[span, :], sem.at[1]))
    count = 0
    for r in range(rows):
        left = 1 - lax.rem(lax.shift_right_logical(bits, r), 2)
        asked[CAP + jnp.where(left > 0, jnp.minimum(count, rows - CAP), rows - CAP)] = r
        count = count + left
    for copy in copies:
        copy.wait()


def signs(meta):
    on = meta[2 * CAP + 1] == 1
    return jnp.where(on, 0.0, 2.0), jnp.where(on, 1.0, -1.0)


def diagonal(square):
    n = square.shape[-1]
    on = lax.broadcasted_iota(jnp.int32, (n, n), 0) == lax.broadcasted_iota(jnp.int32, (n, n), 1)
    return jnp.sum(jnp.where(on, square, 0.0))


def kept(code):
    return lax.rem(jnp.maximum(code, 0), 2).astype(jnp.float32)


def give(stage, out, i, code, sem):
    copy = pltpu.make_async_copy(stage, out.at[i, lax.shift_right_logical(jnp.maximum(code, 0), 1)], sem)

    @pl.when(code >= 0)
    def _():
        copy.start()

    def wait():
        @pl.when(code >= 0)
        def _():
            copy.wait()
    return wait


def near_kernel(meta, own, outer, base_near):
    twice, sign = signs(meta)
    base_near[...] = (twice * outer[...].astype(jnp.float32)
                      + sign * jnp.dot(own[...], outer[...], preferred_element_type=jnp.float32))


def own_kernel(table, meta, asked, meta_inner, own, outer, inner, got_own_hbm, got_far_hbm, out, base_far, turned, trace,
               got_own, got_far, square, side, stage, sem, sem_base, sem_got):
    rows = stage.shape[0]
    block = own.shape[0] // rows
    across = rows + 2 * CAP
    half = CAP * block
    twice, sign = signs(meta)
    left = own[...]
    arrive = []
    for c in range(CAP):
        row = pl.ds(pl.multiple_of(meta[CAP + c] * block, block), block)
        span = pl.ds(c * block, block)
        arrive.append(copy_in(got_far_hbm.at[row, :], got_far.at[span, :], sem_got))
        for d in range(CAP):
            column = pl.ds(pl.multiple_of(meta[CAP + d] * block, block), block)
            arrive.append(copy_in(got_own_hbm.at[row, column], got_own.at[span, pl.ds(d * block, block)], sem_got))
    square[...] = twice * left.astype(jnp.float32) + sign * jnp.dot(left, left, preferred_element_type=jnp.float32)
    for r in range(CAP):
        for c in range(CAP):
            value = outer[pl.ds(pl.multiple_of(asked[c] * block, block), block), pl.ds(r * block, block)]
            turned[pl.ds(r * block, block), pl.ds(c * block, block)] = value.astype(jnp.float32).T.astype(turned.dtype)
    copies = []
    for copy in arrive:
        copy.wait()
    part = sign * jnp.dot(inner[...], got_far[...], preferred_element_type=jnp.float32)
    for c in range(CAP):
        place = pl.ds(pl.multiple_of(meta_inner[CAP + c] * block, block), block)
        square[:, place] = square[:, place] + part[:, c * block:(c + 1) * block]
    for c in range(CAP):
        place = pl.ds(pl.multiple_of(asked[c] * block, block), block)
        copies.append(copy_in(square.at[:, place], base_far.at[:, pl.ds(c * block, block)], sem_base))
    total = jnp.zeros((block, block), jnp.float32)
    for i in range(rows):
        span = pl.ds(i * block, block)
        total = total + kept(table[i * across + i]) * square[span, span]
    trace[0] = diagonal(total)
    side[...] = (twice * inner[...].astype(jnp.float32)
                 + sign * (jnp.dot(left, inner[...], preferred_element_type=jnp.float32)
                           + jnp.dot(inner[...], got_own[...], preferred_element_type=jnp.float32)))
    waits = []
    for i in range(rows):
        span = pl.ds(i * block, block)
        for e in range(rows - CAP):
            k = asked[CAP + e]
            code = table[i * across + k]
            value = square[span, pl.ds(pl.multiple_of(k * block, block), block)]
            stage[i, CAP + e] = (kept(code) * value).astype(stage.dtype)
            waits.append(give(stage.at[i, CAP + e], out, i, code, sem))
        for c in range(CAP):
            code = table[i * across + rows + CAP + c]
            stage[i, c] = (kept(code) * side[span, pl.ds(c * block, block)]).astype(stage.dtype)
            waits.append(give(stage.at[i, c], out, i, code, sem))
    for wait in waits:
        wait()
    for copy in copies:
        copy.wait()


def trace_kernel(rows, table, meta, asked, turned, far_hbm, trace_own, trace, far, sem):
    block = turned.shape[0] // CAP
    across = rows + 2 * CAP
    copy_in(far_hbm, far, sem).wait()
    total = jnp.zeros((8, block), jnp.float32)
    for c in range(CAP):
        mine = asked[c]
        column = pl.ds(c * block, block)
        part = far[:, column].astype(jnp.float32) * turned[:, column].astype(jnp.float32)
        total = total + kept(table[mine * across + mine]) * jnp.sum(part.reshape(CAP * block // 8, 8, block), axis=0)
    value = (trace_own[0] + signs(meta)[1] * jnp.sum(total)) * (1.0 / total_count(rows, block))
    trace[...] = jnp.full(trace.shape, value, jnp.float32)


def total_count(rows, block):
    return rows * block * lax.axis_size(RING)


def last_kernel(table, meta, asked, outer, base_far, base_near, far, near, _, out,
                got, base, stage, sem, sem_base, sem_got):
    rows = stage.shape[0]
    block = outer.shape[0] // rows
    across = rows + 2 * CAP
    half = CAP * block
    arrive = [copy_in(source, got.at[t], sem_got) for t, source in enumerate((far, near))]
    copies = [copy_in(source, base.at[t], sem_base.at[t]) for t, source in enumerate((base_far, base_near))]
    sign = signs(meta)[1].astype(outer.dtype)
    waits = []
    for copy in arrive:
        copy.wait()
    chunk = rows // 2
    for t in range(2):
        right = got[t] * sign
        copies[t].wait()
        for first in range(0, rows, chunk):
            tall = pl.ds(first * block, chunk * block)
            value = base[t, tall, :] + jnp.dot(outer[tall, :], right, preferred_element_type=jnp.float32)
            codes = {}
            for i in range(first, first + chunk):
                for c in range(CAP):
                    code = table[i * across + (asked[c] if t == 0 else rows + c)]
                    codes[i, c] = code
                    low = (i - first) * block
                    stage[i, t * CAP + c] = (kept(code) * value[low:low + block, c * block:(c + 1) * block]).astype(stage.dtype)
            for (i, c), code in codes.items():
                waits.append(give(stage.at[i, t * CAP + c], out, i, code, sem))
    for wait in waits:
        wait()


def body(x, cols, keep, flag):
    rows, slots, block = x.shape[0], x.shape[1], x.shape[2]
    n = lax.axis_size(RING)
    total_rows = rows * n
    bf16, f32, i32 = x.dtype, jnp.float32, jnp.int32
    wide, narrow, across = rows * block, CAP * block, rows + 2 * CAP
    dma = pltpu.SemaphoreType.DMA

    def ints(*shape):
        return pltpu.SMEM(shape, i32)

    def call(kernel, outs, in_specs, scratch, mib, aliases=None, first=None):
        def run(*refs):
            kernel(*(() if first is None else (first,)), *refs)
        return pl.pallas_call(
            run, out_shape=[(pltpu.HBM if len(o) > 3 else jax.ShapeDtypeStruct)(*o[:2]) for o in outs], in_specs=in_specs,
            out_specs=[o[2] for o in outs], scratch_shapes=scratch, name=kernel.__name__,
            input_output_aliases=aliases or {},
            cost_estimate=pl.CostEstimate(flops=1, bytes_accessed=1, transcendentals=0),
            compiler_params=pltpu.CompilerParams(vmem_limit_bytes=mib * MIB))

    inside = [(i, i ^ 1) for i in range(n)]
    upward = [(i, (i + 1) % n) for i in range(1, n, 2)]
    outside = upward + [(b, a) for a, b in upward]
    hbm = functools.partial(pltpu.with_memory_space_constraint, memory_space=pltpu.HBM)
    barrier = lax.optimization_barrier

    cols_outer = permute(cols, outside)
    own, outer, inner, table, meta = call(
        spread_kernel,
        [((wide, wide), bf16, VMEM), ((wide, narrow), bf16, VMEM), ((wide, narrow), bf16, VMEM),
         ((rows * across,), i32, SMEM), ((2 * CAP + 2,), i32, SMEM)],
        [HBM] * 2 + [SMEM, HBM], [ints(rows, slots), ints(rows, slots), pltpu.VMEM(x.shape, bf16), ints(rows * 3 * rows),
                    ints(2 * (CAP + 1)), dma((2 + rows,))], 16, first=total_rows)(hbm(cols), hbm(keep), flag, hbm(x))
    far_out, near_out, asked = call(
        pack_kernel,
        [((narrow, narrow), bf16, HBM), ((narrow, narrow), bf16, HBM), ((CAP + rows - CAP + 1,), i32, SMEM)],
        [SMEM] * 2 + [VMEM] * 2, [ints(CAP + 1), pltpu.VMEM((narrow, 2 * narrow), bf16), dma((2,))], 16,
    )(meta, cols_outer, own, outer)
    far = permute(far_out, outside)
    meta, asked = barrier((meta, asked))
    base_near, = call(near_kernel, [((wide, narrow), f32, VMEM)], [SMEM] + [VMEM] * 2, [], 12)(meta, own, outer)
    base_near, own_there, inner_there, meta_there = barrier((base_near, own, inner, meta))
    got_own, got_far, meta_inner = (permute(v, inside) for v in (own_there, inner_there, meta_there))
    out, base_far, turned, trace_own = call(
        own_kernel,
        [(x.shape, bf16, HBM), ((wide, narrow), f32, HBM, True), ((narrow, narrow), bf16, VMEM), ((1,), f32, SMEM)],
        [SMEM] * 4 + [VMEM] * 3 + [HBM] * 2,
        [pltpu.VMEM((narrow, narrow), bf16), pltpu.VMEM((narrow, narrow), bf16), pltpu.VMEM((wide, wide), f32),
         pltpu.VMEM((wide, narrow), f32), pltpu.VMEM((rows, rows, block, block), bf16), dma, dma, dma], 24,
    )(table, meta, asked, meta_inner, own, outer, inner, got_own, got_far)
    partial, = call(
        trace_kernel, [((8, block), f32, VMEM)], [SMEM] * 3 + [VMEM, HBM, SMEM],
        [pltpu.VMEM((narrow, narrow), bf16), dma], 12, first=rows)(table, meta, asked, turned, far, trace_own)
    near_out, partial = barrier((near_out, partial))
    near = permute(near_out, outside)
    total = ring_sum(partial)
    out, total = barrier((out, total))
    out, = call(
        last_kernel, [(x.shape, bf16, HBM)], [SMEM] * 3 + [VMEM] + [HBM] * 5,
        [pltpu.VMEM((2, narrow, narrow), bf16), pltpu.VMEM((2, wide, narrow), f32),
         pltpu.VMEM((rows, 2 * CAP, block, block), bf16), dma, dma((2,)), dma], 24, {8: 0},
    )(table, meta, asked, outer, hbm(base_far), base_near, far, near, out)
    return out, total[0, :1]


def solution(mesh):
    placed = (
        P(("groups", "row", "col"), None, None, None),
        P(("groups", "row", "col"), None),
        P(("groups", "row", "col"), None),
        P("groups"),
    )
    return jax.shard_map(
        body,
        mesh=mesh,
        in_specs=placed,
        out_specs=(P(("groups", "row", "col"), None, None, None), P("groups")),
        check_vma=False,
    )
```

```python
import functools

import jax
import jax.numpy as jnp
from jax import lax
from jax.experimental import pallas as pl
from jax.experimental.pallas import tpu as pltpu
from jax.sharding import PartitionSpec as P

CAP = 4
RING = ("row", "col")
SMEM = pl.BlockSpec(memory_space=pltpu.SMEM)
VMEM = pl.BlockSpec(memory_space=pltpu.VMEM)
HBM = pl.BlockSpec(memory_space=pltpu.HBM)
MIB = 1024 * 1024


def permute(value, pairs):
    return lax.ppermute(value, RING, pairs)


def ring_steps():
    n, cols = lax.axis_size(RING), lax.axis_size("col")
    if n & (n - 1) or cols & (cols - 1) or cols < 4:
        return None
    return [1] + [cols << k for k in range((n // cols).bit_length() - 1)] + [2 << k for k in range(cols.bit_length() - 2)]


def partner(value, step):
    return permute(value, [(i, i ^ step) for i in range(lax.axis_size(RING))])


def rank(bits, rows, order, first):
    count = 0
    for r in range(rows):
        named = lax.rem(lax.shift_right_logical(bits, r), 2)
        order[first + jnp.where(named > 0, jnp.minimum(count, CAP), CAP)] = r
        count = count + named


def clear(ref, count, value):
    for q in range(count):
        ref[q] = value


def copy_in(source, target, sem):
    copy = pltpu.make_async_copy(source, target, sem)
    copy.start()
    return copy


def spread_kernel(total_rows, cols_hbm, keep_hbm, flag, x_hbm, own, outer, inner, table, meta,
                  cols, keep, x, slots_of, order, sem):
    rows, slots = cols.shape
    block = x.shape[-1]
    wide = 3 * rows
    across = rows + 2 * CAP
    lists = [copy_in(cols_hbm, cols, sem.at[0]), copy_in(keep_hbm, keep, sem.at[1])]
    blocks = [copy_in(x_hbm.at[i], x.at[i], sem.at[2 + i]) for i in range(rows)]
    clear(slots_of, rows * wide, -1)
    for copy in lists:
        copy.wait()
    base = cols[0, 0]
    odd = lax.rem(lax.div(base, rows), 2)
    ahead = jnp.where(odd == 1, 0, rows)
    behind = jnp.where(odd == 1, 2 * rows, rows) - (total_rows - rows)
    bits = 0
    for i in range(rows):
        for s in range(slots):
            rel = cols[i, s] - base
            rel = jnp.where(rel < 0, rel + total_rows, rel)
            rel = rel + jnp.where(rel >= 2 * rows, behind, jnp.where(rel >= rows, ahead, 0))
            slots_of[i * wide + rel] = 2 * s + keep[i, s]
            bits = bits | lax.shift_left(1, rel)
    rank(lax.shift_right_logical(bits, rows), rows, order, 0)
    rank(lax.shift_right_logical(bits, 2 * rows), rows, order, CAP + 1)
    for c in range(2 * CAP):
        meta[c] = order[c + c // CAP]
    meta[2 * CAP] = base
    meta[2 * CAP + 1] = flag[0]
    for i in range(rows):
        span = pl.ds(i * block, block)
        blocks[i].wait()
        for k in range(rows):
            code = slots_of[i * wide + k]
            table[i * across + k] = code
            own[span, pl.ds(k * block, block)] = x[i, lax.shift_right_logical(code, 1)]
        for first, target, start, shift in ((0, outer, rows, 0), (CAP + 1, inner, 2 * rows, CAP)):
            for c in range(CAP):
                code = slots_of[i * wide + start + order[first + c]]
                table[i * across + rows + shift + c] = code
                value = x[i, lax.shift_right_logical(jnp.maximum(code, 0), 1)]
                target[span, pl.ds(c * block, block)] = jnp.where(code >= 0, value, jnp.zeros_like(value))


def pack_kernel(meta, cols_outer, own, outer, far_out, near_out, asked, order):
    rows, slots = cols_outer.shape
    block = own.shape[0] // rows
    base = meta[2 * CAP]
    bits = 0
    for i in range(rows):
        for s in range(slots):
            rel = cols_outer[i, s] - base
            bits = bits | lax.shift_left(1, jnp.where((rel >= 0) & (rel < rows), rel, rows))
    rank(bits, rows, order, 0)
    for a in range(CAP):
        asked[a] = order[a]
        span = pl.ds(a * block, block)
        row = pl.ds(pl.multiple_of(order[a] * block, block), block)
        far_out[span, :] = outer[row, :]
        for b in range(CAP):
            column = pl.ds(pl.multiple_of(order[b] * block, block), block)
            near_out[span, pl.ds(b * block, block)] = own[row, column]
    count = 0
    for r in range(rows):
        left = 1 - lax.rem(lax.shift_right_logical(bits, r), 2)
        asked[CAP + jnp.where(left > 0, jnp.minimum(count, rows - CAP), rows - CAP)] = r
        count = count + left


def signs(meta):
    on = meta[2 * CAP + 1] == 1
    return jnp.where(on, 0.0, 2.0), jnp.where(on, 1.0, -1.0)


def diagonal(square):
    n = square.shape[-1]
    on = lax.broadcasted_iota(jnp.int32, (n, n), 0) == lax.broadcasted_iota(jnp.int32, (n, n), 1)
    return jnp.sum(jnp.where(on, square, 0.0))


def kept(code):
    return lax.rem(jnp.maximum(code, 0), 2).astype(jnp.float32)


def give(stage, out, i, code, sem):
    copy = pltpu.make_async_copy(stage, out.at[i, lax.shift_right_logical(jnp.maximum(code, 0), 1)], sem)

    @pl.when(code >= 0)
    def _():
        copy.start()

    def wait():
        @pl.when(code >= 0)
        def _():
            copy.wait()
    return wait


def own_kernel(table, meta, asked, cols_inner, own, outer, inner, x_inner, out, base_far, base_near, turned, trace,
               got_own, got_far, square, side, stage, slots_of, order, sem, sem_base, sem_got):
    rows, slots = cols_inner.shape
    block = own.shape[0] // rows
    across = rows + 2 * CAP
    twice, sign = signs(meta)
    left = own[...]
    left_signed = left * sign.astype(left.dtype)
    inner_signed = inner[...] * sign.astype(left.dtype)
    wide = 2 * rows + 1
    clear(slots_of, rows * wide, -1)
    mine, theirs = meta[2 * CAP], cols_inner[0, 0]
    bits = 0
    for i in range(rows):
        for s in range(slots):
            near = cols_inner[i, s] - theirs
            far = cols_inner[i, s] - mine
            far = jnp.where((far >= 0) & (far < rows), far, rows)
            bits = bits | lax.shift_left(1, far)
            slots_of[i * wide + jnp.where((near >= 0) & (near < rows), near, rows + far)] = s
    rank(bits, rows, order, 0)
    arrive = []
    for r in range(CAP):
        row = meta[CAP + r]
        span = pl.ds(r * block, block)
        for c in range(CAP):
            place = pl.ds(c * block, block)
            slot = slots_of[row * wide + meta[CAP + c]]
            arrive.append(copy_in(x_inner.at[row, jnp.maximum(slot, 0)], got_own.at[span, place], sem_got))
            slot = slots_of[row * wide + rows + order[c]]
            far_slot = jnp.maximum(slot, 0)
            arrive.append(copy_in(x_inner.at[row, far_slot], got_far.at[span, place], sem_got))
    base_near[...] = (twice * outer[...].astype(jnp.float32)
                      + jnp.dot(left_signed, outer[...], preferred_element_type=jnp.float32))
    square[...] = twice * left.astype(jnp.float32) + jnp.dot(left_signed, left, preferred_element_type=jnp.float32)
    for r in range(CAP):
        for c in range(CAP):
            value = outer[pl.ds(pl.multiple_of(asked[c] * block, block), block), pl.ds(r * block, block)]
            turned[pl.ds(r * block, block), pl.ds(c * block, block)] = value.T
    copies = []
    for copy in arrive:
        copy.wait()
    for r in range(CAP):
        for c in range(CAP):
            @pl.when(slots_of[meta[CAP + r] * wide + rows + order[c]] < 0)
            def _():
                got_far[pl.ds(r * block, block), pl.ds(c * block, block)] = jnp.zeros((block, block), got_far.dtype)
    part = jnp.dot(inner_signed, got_far[...], preferred_element_type=jnp.float32)
    for c in range(CAP):
        place = pl.ds(pl.multiple_of(order[c] * block, block), block)
        square[:, place] = square[:, place] + part[:, c * block:(c + 1) * block]
    for c in range(CAP):
        place = pl.ds(pl.multiple_of(asked[c] * block, block), block)
        copies.append(copy_in(square.at[:, place], base_far.at[:, pl.ds(c * block, block)], sem_base))
    total = jnp.zeros((block, block), jnp.float32)
    for i in range(rows):
        span = pl.ds(i * block, block)
        total = total + kept(table[i * across + i]) * square[span, span]
    trace[0] = diagonal(total)
    side[...] = twice * inner[...].astype(jnp.float32) + jnp.dot(
        jnp.concatenate([left_signed, inner_signed], axis=1), jnp.concatenate([inner[...], got_own[...]], axis=0),
        preferred_element_type=jnp.float32)
    waits = []
    for i in range(rows):
        span = pl.ds(i * block, block)
        for e in range(rows - CAP):
            k = asked[CAP + e]
            code = table[i * across + k]
            value = square[span, pl.ds(pl.multiple_of(k * block, block), block)]
            stage[i, CAP + e] = (kept(code) * value).astype(stage.dtype)
            waits.append(give(stage.at[i, CAP + e], out, i, code, sem))
        for c in range(CAP):
            code = table[i * across + rows + CAP + c]
            stage[i, c] = (kept(code) * side[span, pl.ds(c * block, block)]).astype(stage.dtype)
            waits.append(give(stage.at[i, c], out, i, code, sem))
    for wait in waits:
        wait()
    for copy in copies:
        copy.wait()


def trace_kernel(rows, table, meta, asked, turned, far_hbm, trace_own, trace, far, sem):
    block = turned.shape[0] // CAP
    across = rows + 2 * CAP
    copy_in(far_hbm, far, sem).wait()
    total = jnp.zeros((8, block), jnp.float32)
    for c in range(CAP):
        mine = asked[c]
        column = pl.ds(c * block, block)
        part = far[:, column].astype(jnp.float32) * turned[:, column].astype(jnp.float32)
        total = total + kept(table[mine * across + mine]) * jnp.sum(part.reshape(CAP * block // 8, 8, block), axis=0)
    value = (trace_own[0] + signs(meta)[1] * jnp.sum(total)) * (1.0 / total_count(rows, block))
    trace[...] = jnp.full(trace.shape, value, jnp.float32)


def total_count(rows, block):
    return rows * block * lax.axis_size(RING)


def finish_half(near, rows, table, meta, asked, outer, base_hbm, got_hbm, out, got, base, stage, sem, sem_base, sem_got):
    block = outer.shape[0] // rows
    across = rows + 2 * CAP
    arrive = copy_in(got_hbm, got, sem_got)
    copy = copy_in(base_hbm, base, sem_base)
    arrive.wait()
    right = got[...] * signs(meta)[1].astype(got.dtype)
    copy.wait()
    waits = []
    chunk = rows // 2
    for first in range(0, rows, chunk):
        tall = pl.ds(first * block, chunk * block)
        value = base[tall, :] + jnp.dot(outer[tall, :], right, preferred_element_type=jnp.float32)
        codes = {}
        for i in range(first, first + chunk):
            low = (i - first) * block
            for c in range(CAP):
                code = table[i * across + (rows + c if near else asked[c])]
                codes[i, c] = code
                stage[i, c] = (kept(code) * value[low:low + block, c * block:(c + 1) * block]).astype(stage.dtype)
        for (i, c), code in codes.items():
            waits.append(give(stage.at[i, c], out, i, code, sem))
    for wait in waits:
        wait()


def far_kernel(rows, table, meta, asked, outer, base, far, _, out, *scratch):
    finish_half(False, rows, table, meta, asked, outer, base, far, out, *scratch)


def last_kernel(rows, table, meta, asked, outer, base, near, _, out, *scratch):
    finish_half(True, rows, table, meta, asked, outer, base, near, out, *scratch)


def body(x, cols, keep, flag):
    rows, slots, block = x.shape[0], x.shape[1], x.shape[2]
    n = lax.axis_size(RING)
    total_rows = rows * n
    bf16, f32, i32 = x.dtype, jnp.float32, jnp.int32
    wide, narrow, across = rows * block, CAP * block, rows + 2 * CAP
    dma = pltpu.SemaphoreType.DMA

    def ints(*shape):
        return pltpu.SMEM(shape, i32)

    def call(kernel, outs, in_specs, scratch, mib, aliases=None, first=None):
        def run(*refs):
            kernel(*(() if first is None else (first,)), *refs)
        return pl.pallas_call(
            run, out_shape=[(pltpu.HBM if len(o) > 3 else jax.ShapeDtypeStruct)(*o[:2]) for o in outs], in_specs=in_specs,
            out_specs=[o[2] for o in outs], scratch_shapes=scratch, name=kernel.__name__,
            input_output_aliases=aliases or {},
            cost_estimate=pl.CostEstimate(flops=1, bytes_accessed=1, transcendentals=0),
            compiler_params=pltpu.CompilerParams(vmem_limit_bytes=mib * MIB))

    inside = [(i, i ^ 1) for i in range(n)]
    upward = [(i, (i + 1) % n) for i in range(1, n, 2)]
    outside = upward + [(b, a) for a, b in upward]
    hbm = functools.partial(pltpu.with_memory_space_constraint, memory_space=pltpu.HBM)
    barrier = lax.optimization_barrier

    x_inner = permute(x, inside)
    cols_inner = permute(cols, inside)
    cols_outer = permute(cols, outside)
    own, outer, inner, table, meta = call(
        spread_kernel,
        [((wide, wide), bf16, VMEM), ((wide, narrow), bf16, VMEM), ((wide, narrow), bf16, VMEM),
         ((rows * across,), i32, SMEM), ((2 * CAP + 2,), i32, SMEM)],
        [HBM] * 2 + [SMEM, HBM], [ints(rows, slots), ints(rows, slots), pltpu.VMEM(x.shape, bf16), ints(rows * 3 * rows),
                    ints(2 * (CAP + 1)), dma((2 + rows,))], 16, first=total_rows)(hbm(cols), hbm(keep), flag, hbm(x))
    far_out, near_out, asked = call(
        pack_kernel,
        [((narrow, narrow), bf16, VMEM), ((narrow, narrow), bf16, VMEM), ((CAP + rows - CAP + 1,), i32, SMEM)],
        [SMEM] * 2 + [VMEM] * 2, [ints(CAP + 1)], 16,
    )(meta, cols_outer, own, outer)
    far = permute(far_out, outside)
    out, base_far, base_near, turned, trace_own = call(
        own_kernel,
        [(x.shape, bf16, HBM), ((wide, narrow), f32, HBM, True), ((wide, narrow), f32, VMEM),
         ((narrow, narrow), bf16, VMEM), ((1,), f32, SMEM)],
        [SMEM] * 4 + [VMEM] * 3 + [HBM],
        [pltpu.VMEM((narrow, narrow), bf16), pltpu.VMEM((narrow, narrow), bf16), pltpu.VMEM((wide, wide), f32),
         pltpu.VMEM((wide, narrow), f32), pltpu.VMEM((rows, rows, block, block), bf16), ints(rows * (2 * rows + 1)),
         ints(CAP + 1), dma, dma, dma], 24)(table, meta, asked, cols_inner, own, outer, inner, x_inner)
    partial, = call(
        trace_kernel, [((8, block), f32, VMEM)], [SMEM] * 3 + [VMEM, HBM, SMEM],
        [pltpu.VMEM((narrow, narrow), bf16), dma], 12, first=rows)(table, meta, asked, turned, far, trace_own)
    near_out, partial = barrier((near_out, partial))
    near = permute(near_out, outside)
    half_scratch = [pltpu.VMEM((narrow, narrow), bf16), pltpu.VMEM((wide, narrow), f32),
                    pltpu.VMEM((rows, CAP, block, block), bf16), dma, dma, dma]

    def half(kernel, base, got, out):
        result, = call(
            kernel, [(x.shape, bf16, HBM)], [SMEM] * 3 + [VMEM] + [HBM] * 3, half_scratch, 16, {6: 0}, first=rows,
        )(table, meta, asked, outer, base, got, out)
        return result

    steps = ring_steps()
    if steps is None:
        total = lax.psum(partial, RING)
        return half(last_kernel, base_near, near, half(far_kernel, hbm(base_far), far, out)), total[0, :1]
    partial = partial + partner(partial, steps[0])
    out, partial = barrier((out, partial))
    out = half(far_kernel, hbm(base_far), far, out)
    out, partial = barrier((out, partial))
    for step in steps[1:-1]:
        partial = partial + partner(partial, step)
    ready, partial = barrier((out, partial))
    out = half(last_kernel, base_near, near, ready)
    other, out = barrier((partner(partial, steps[-1]), out))
    return out, (partial + other)[0, :1]


def solution(mesh):
    placed = (
        P(("groups", "row", "col"), None, None, None),
        P(("groups", "row", "col"), None),
        P(("groups", "row", "col"), None),
        P("groups"),
    )
    return jax.shard_map(
        body,
        mesh=mesh,
        in_specs=placed,
        out_specs=(P(("groups", "row", "col"), None, None, None), P("groups")),
        check_vma=False,
    )
```

```python
import functools

import jax
import jax.numpy as jnp
from jax import lax
from jax.experimental import pallas as pl
from jax.experimental.pallas import tpu as pltpu
from jax.sharding import PartitionSpec as P

CAP = 4
RING = ("row", "col")
SMEM = pl.BlockSpec(memory_space=pltpu.SMEM)
VMEM = pl.BlockSpec(memory_space=pltpu.VMEM)
HBM = pl.BlockSpec(memory_space=pltpu.HBM)
MIB = 1024 * 1024


def permute(value, pairs):
    return lax.ppermute(value, RING, pairs)


def ring_steps():
    n, cols = lax.axis_size(RING), lax.axis_size("col")
    if n & (n - 1) or cols & (cols - 1) or cols < 4:
        return None
    return [1] + [cols << k for k in range((n // cols).bit_length() - 1)] + [2 << k for k in range(cols.bit_length() - 2)]


def partner(value, step):
    return permute(value, [(i, i ^ step) for i in range(lax.axis_size(RING))])


def rank(bits, rows, order, first):
    count = 0
    for r in range(rows):
        named = lax.rem(lax.shift_right_logical(bits, r), 2)
        order[first + jnp.where(named > 0, jnp.minimum(count, CAP), CAP)] = r
        count = count + named


def clear(ref, count, value):
    for q in range(count):
        ref[q] = value


def copy_in(source, target, sem):
    copy = pltpu.make_async_copy(source, target, sem)
    copy.start()
    return copy


def spread_kernel(total_rows, cols_hbm, keep_hbm, flag, x_hbm, own, outer, inner, table, meta,
                  cols, keep, x, slots_of, order, sem):
    rows, slots = cols.shape
    block = x.shape[-1]
    wide = 3 * rows
    across = rows + 2 * CAP
    lists = [copy_in(cols_hbm, cols, sem.at[0]), copy_in(keep_hbm, keep, sem.at[1])]
    blocks = [copy_in(x_hbm.at[i], x.at[i], sem.at[2 + i]) for i in range(rows)]
    clear(slots_of, rows * wide, -1)
    for copy in lists:
        copy.wait()
    base = cols[0, 0]
    odd = lax.rem(lax.div(base, rows), 2)
    ahead = jnp.where(odd == 1, 0, rows)
    behind = jnp.where(odd == 1, 2 * rows, rows) - (total_rows - rows)
    bits = 0
    for i in range(rows):
        for s in range(slots):
            rel = cols[i, s] - base
            rel = jnp.where(rel < 0, rel + total_rows, rel)
            rel = rel + jnp.where(rel >= 2 * rows, behind, jnp.where(rel >= rows, ahead, 0))
            slots_of[i * wide + rel] = 2 * s + keep[i, s]
            bits = bits | lax.shift_left(1, rel)
    rank(lax.shift_right_logical(bits, rows), rows, order, 0)
    rank(lax.shift_right_logical(bits, 2 * rows), rows, order, CAP + 1)
    for c in range(2 * CAP):
        meta[c] = order[c + c // CAP]
    meta[2 * CAP] = base
    meta[2 * CAP + 1] = flag[0]
    for i in range(rows):
        span = pl.ds(i * block, block)
        blocks[i].wait()
        for k in range(rows):
            code = slots_of[i * wide + k]
            table[i * across + k] = code
            own[span, pl.ds(k * block, block)] = x[i, lax.shift_right_logical(code, 1)]
        for first, target, start, shift in ((0, outer, rows, 0), (CAP + 1, inner, 2 * rows, CAP)):
            for c in range(CAP):
                code = slots_of[i * wide + start + order[first + c]]
                table[i * across + rows + shift + c] = code
                value = x[i, lax.shift_right_logical(jnp.maximum(code, 0), 1)]
                target[span, pl.ds(c * block, block)] = jnp.where(code >= 0, value, jnp.zeros_like(value))


def pack_kernel(meta, cols_outer, own, outer, far_out, near_out, asked, order):
    rows, slots = cols_outer.shape
    block = own.shape[0] // rows
    base = meta[2 * CAP]
    bits = 0
    for i in range(rows):
        for s in range(slots):
            rel = cols_outer[i, s] - base
            bits = bits | lax.shift_left(1, jnp.where((rel >= 0) & (rel < rows), rel, rows))
    rank(bits, rows, order, 0)
    for a in range(CAP):
        asked[a] = order[a]
        span = pl.ds(a * block, block)
        row = pl.ds(pl.multiple_of(order[a] * block, block), block)
        far_out[span, :] = outer[row, :]
        for b in range(CAP):
            column = pl.ds(pl.multiple_of(order[b] * block, block), block)
            near_out[span, pl.ds(b * block, block)] = own[row, column]
    count = 0
    for r in range(rows):
        left = 1 - lax.rem(lax.shift_right_logical(bits, r), 2)
        asked[CAP + jnp.where(left > 0, jnp.minimum(count, rows - CAP), rows - CAP)] = r
        count = count + left


def signs(meta):
    on = meta[2 * CAP + 1] == 1
    return jnp.where(on, 0.0, 2.0), jnp.where(on, 1.0, -1.0)


def diagonal(square):
    n = square.shape[-1]
    on = lax.broadcasted_iota(jnp.int32, (n, n), 0) == lax.broadcasted_iota(jnp.int32, (n, n), 1)
    return jnp.sum(jnp.where(on, square, 0.0))


def kept(code):
    return lax.rem(jnp.maximum(code, 0), 2).astype(jnp.float32)


def give(stage, out, i, code, sem):
    copy = pltpu.make_async_copy(stage, out.at[i, lax.shift_right_logical(jnp.maximum(code, 0), 1)], sem)

    @pl.when(code >= 0)
    def _():
        copy.start()

    def wait():
        @pl.when(code >= 0)
        def _():
            copy.wait()
    return wait


def own_kernel(table, meta, asked, cols_inner, own, outer, inner, x_inner, out, base_far, base_near, turned, trace,
               got_own, got_far, square, side, stage, slots_of, order, sem, sem_got):
    rows, slots = cols_inner.shape
    block = own.shape[0] // rows
    across = rows + 2 * CAP
    twice, sign = signs(meta)
    left = own[...]
    left_signed = left * sign.astype(left.dtype)
    inner_signed = inner[...] * sign.astype(left.dtype)
    wide = 2 * rows + 1
    clear(slots_of, rows * wide, -1)
    mine, theirs = meta[2 * CAP], cols_inner[0, 0]
    bits = 0
    for i in range(rows):
        for s in range(slots):
            near = cols_inner[i, s] - theirs
            far = cols_inner[i, s] - mine
            far = jnp.where((far >= 0) & (far < rows), far, rows)
            bits = bits | lax.shift_left(1, far)
            slots_of[i * wide + jnp.where((near >= 0) & (near < rows), near, rows + far)] = s
    rank(bits, rows, order, 0)
    arrive = []
    for r in range(CAP):
        row = meta[CAP + r]
        span = pl.ds(r * block, block)
        for c in range(CAP):
            place = pl.ds(c * block, block)
            slot = slots_of[row * wide + meta[CAP + c]]
            arrive.append(copy_in(x_inner.at[row, jnp.maximum(slot, 0)], got_own.at[span, place], sem_got))
            slot = slots_of[row * wide + rows + order[c]]
            far_slot = jnp.maximum(slot, 0)
            arrive.append(copy_in(x_inner.at[row, far_slot], got_far.at[span, place], sem_got))
    base_near[...] = (twice * outer[...].astype(jnp.float32)
                      + jnp.dot(left_signed, outer[...], preferred_element_type=jnp.float32))
    square[...] = twice * left.astype(jnp.float32) + jnp.dot(left_signed, left, preferred_element_type=jnp.float32)
    for r in range(CAP):
        for c in range(CAP):
            value = outer[pl.ds(pl.multiple_of(asked[c] * block, block), block), pl.ds(r * block, block)]
            turned[pl.ds(r * block, block), pl.ds(c * block, block)] = value.T
    for copy in arrive:
        copy.wait()
    for r in range(CAP):
        for c in range(CAP):
            @pl.when(slots_of[meta[CAP + r] * wide + rows + order[c]] < 0)
            def _():
                got_far[pl.ds(r * block, block), pl.ds(c * block, block)] = jnp.zeros((block, block), got_far.dtype)
    part = jnp.dot(inner_signed, got_far[...], preferred_element_type=jnp.float32)
    for c in range(CAP):
        place = pl.ds(pl.multiple_of(order[c] * block, block), block)
        square[:, place] = square[:, place] + part[:, c * block:(c + 1) * block]
    for c in range(CAP):
        place = pl.ds(pl.multiple_of(asked[c] * block, block), block)
        base_far[:, pl.ds(c * block, block)] = square[:, place]
    total = jnp.zeros((block, block), jnp.float32)
    for i in range(rows):
        span = pl.ds(i * block, block)
        total = total + kept(table[i * across + i]) * square[span, span]
    trace[0] = diagonal(total)
    side[...] = twice * inner[...].astype(jnp.float32) + jnp.dot(
        jnp.concatenate([left_signed, inner_signed], axis=1), jnp.concatenate([inner[...], got_own[...]], axis=0),
        preferred_element_type=jnp.float32)
    waits = []
    for i in range(rows):
        span = pl.ds(i * block, block)
        for e in range(rows - CAP):
            k = asked[CAP + e]
            code = table[i * across + k]
            value = square[span, pl.ds(pl.multiple_of(k * block, block), block)]
            stage[i, CAP + e] = (kept(code) * value).astype(stage.dtype)
            waits.append(give(stage.at[i, CAP + e], out, i, code, sem))
        for c in range(CAP):
            code = table[i * across + rows + CAP + c]
            stage[i, c] = (kept(code) * side[span, pl.ds(c * block, block)]).astype(stage.dtype)
            waits.append(give(stage.at[i, c], out, i, code, sem))
    for wait in waits:
        wait()


def trace_kernel(rows, table, meta, asked, turned, far_hbm, trace_own, trace, far, sem):
    block = turned.shape[0] // CAP
    across = rows + 2 * CAP
    copy_in(far_hbm, far, sem).wait()
    total = jnp.zeros((8, block), jnp.float32)
    for c in range(CAP):
        mine = asked[c]
        column = pl.ds(c * block, block)
        part = far[:, column].astype(jnp.float32) * turned[:, column].astype(jnp.float32)
        total = total + kept(table[mine * across + mine]) * jnp.sum(part.reshape(CAP * block // 8, 8, block), axis=0)
    value = (trace_own[0] + signs(meta)[1] * jnp.sum(total)) * (1.0 / total_count(rows, block))
    trace[...] = jnp.full(trace.shape, value, jnp.float32)


def total_count(rows, block):
    return rows * block * lax.axis_size(RING)


def finish_half(near, rows, table, meta, asked, outer, base_hbm, got_hbm, out, got, base, stage, sem, sem_base, sem_got):
    block = outer.shape[0] // rows
    across = rows + 2 * CAP
    arrive = copy_in(got_hbm, got, sem_got)
    copy = copy_in(base_hbm, base, sem_base)
    arrive.wait()
    right = got[...] * signs(meta)[1].astype(got.dtype)
    copy.wait()
    waits = []
    chunk = rows // 2
    for first in range(0, rows, chunk):
        tall = pl.ds(first * block, chunk * block)
        value = base[tall, :] + jnp.dot(outer[tall, :], right, preferred_element_type=jnp.float32)
        codes = {}
        for i in range(first, first + chunk):
            low = (i - first) * block
            for c in range(CAP):
                code = table[i * across + (rows + c if near else asked[c])]
                codes[i, c] = code
                stage[i, c] = (kept(code) * value[low:low + block, c * block:(c + 1) * block]).astype(stage.dtype)
        for (i, c), code in codes.items():
            waits.append(give(stage.at[i, c], out, i, code, sem))
    for wait in waits:
        wait()


def far_kernel(rows, table, meta, asked, outer, base, far, _, out, *scratch):
    finish_half(False, rows, table, meta, asked, outer, base, far, out, *scratch)


def last_kernel(rows, table, meta, asked, outer, base, near, _, out, *scratch):
    finish_half(True, rows, table, meta, asked, outer, base, near, out, *scratch)


def body(x, cols, keep, flag):
    rows, slots, block = x.shape[0], x.shape[1], x.shape[2]
    n = lax.axis_size(RING)
    total_rows = rows * n
    bf16, f32, i32 = x.dtype, jnp.float32, jnp.int32
    wide, narrow, across = rows * block, CAP * block, rows + 2 * CAP
    dma = pltpu.SemaphoreType.DMA

    def ints(*shape):
        return pltpu.SMEM(shape, i32)

    def call(kernel, outs, in_specs, scratch, mib, aliases=None, first=None):
        def run(*refs):
            kernel(*(() if first is None else (first,)), *refs)
        return pl.pallas_call(
            run, out_shape=[(pltpu.HBM if len(o) > 3 else jax.ShapeDtypeStruct)(*o[:2]) for o in outs], in_specs=in_specs,
            out_specs=[o[2] for o in outs], scratch_shapes=scratch, name=kernel.__name__,
            input_output_aliases=aliases or {},
            cost_estimate=pl.CostEstimate(flops=1, bytes_accessed=1, transcendentals=0),
            compiler_params=pltpu.CompilerParams(vmem_limit_bytes=mib * MIB))

    inside = [(i, i ^ 1) for i in range(n)]
    upward = [(i, (i + 1) % n) for i in range(1, n, 2)]
    outside = upward + [(b, a) for a, b in upward]
    hbm = functools.partial(pltpu.with_memory_space_constraint, memory_space=pltpu.HBM)
    barrier = lax.optimization_barrier

    x_inner = permute(x, inside)
    cols_inner = permute(cols, inside)
    cols_outer = permute(cols, outside)
    own, outer, inner, table, meta = call(
        spread_kernel,
        [((wide, wide), bf16, VMEM), ((wide, narrow), bf16, VMEM), ((wide, narrow), bf16, VMEM),
         ((rows * across,), i32, SMEM), ((2 * CAP + 2,), i32, SMEM)],
        [HBM] * 2 + [SMEM, HBM], [ints(rows, slots), ints(rows, slots), pltpu.VMEM(x.shape, bf16), ints(rows * 3 * rows),
                    ints(2 * (CAP + 1)), dma((2 + rows,))], 16, first=total_rows)(hbm(cols), hbm(keep), flag, hbm(x))
    far_out, near_out, asked = call(
        pack_kernel,
        [((narrow, narrow), bf16, VMEM), ((narrow, narrow), bf16, VMEM), ((CAP + rows - CAP + 1,), i32, SMEM)],
        [SMEM] * 2 + [VMEM] * 2, [ints(CAP + 1)], 16,
    )(meta, cols_outer, own, outer)
    far = permute(far_out, outside)
    out, base_far, base_near, turned, trace_own = call(
        own_kernel,
        [(x.shape, bf16, HBM), ((wide, narrow), f32, VMEM), ((wide, narrow), f32, VMEM),
         ((narrow, narrow), bf16, VMEM), ((1,), f32, SMEM)],
        [SMEM] * 4 + [VMEM] * 3 + [HBM],
        [pltpu.VMEM((narrow, narrow), bf16), pltpu.VMEM((narrow, narrow), bf16), pltpu.VMEM((wide, wide), f32),
         pltpu.VMEM((wide, narrow), f32), pltpu.VMEM((rows, rows, block, block), bf16), ints(rows * (2 * rows + 1)),
         ints(CAP + 1), dma, dma], 24)(table, meta, asked, cols_inner, own, outer, inner, x_inner)
    partial, = call(
        trace_kernel, [((8, block), f32, VMEM)], [SMEM] * 3 + [VMEM, HBM, SMEM],
        [pltpu.VMEM((narrow, narrow), bf16), dma], 12, first=rows)(table, meta, asked, turned, far, trace_own)
    near_out, partial = barrier((near_out, partial))
    near = permute(near_out, outside)
    half_scratch = [pltpu.VMEM((narrow, narrow), bf16), pltpu.VMEM((wide, narrow), f32),
                    pltpu.VMEM((rows, CAP, block, block), bf16), dma, dma, dma]

    def half(kernel, base, got, out):
        result, = call(
            kernel, [(x.shape, bf16, HBM)], [SMEM] * 3 + [VMEM] + [HBM] * 3, half_scratch, 16, {6: 0}, first=rows,
        )(table, meta, asked, outer, base, got, out)
        return result

    steps = ring_steps()
    if steps is None:
        total = lax.psum(partial, RING)
        return half(last_kernel, base_near, near, half(far_kernel, base_far, far, out)), total[0, :1]
    partial = partial + partner(partial, steps[0])
    out, partial = barrier((out, partial))
    out = half(far_kernel, base_far, far, out)
    out, partial = barrier((out, partial))
    for step in steps[1:-1]:
        partial = partial + partner(partial, step)
    ready, partial = barrier((out, partial))
    out = half(last_kernel, base_near, near, ready)
    other, out = barrier((partner(partial, steps[-1] | 1), out))
    return out, (partial + other)[0, :1]


def solution(mesh):
    placed = (
        P(("groups", "row", "col"), None, None, None),
        P(("groups", "row", "col"), None),
        P(("groups", "row", "col"), None),
        P("groups"),
    )
    return jax.shard_map(
        body,
        mesh=mesh,
        in_specs=placed,
        out_specs=(P(("groups", "row", "col"), None, None, None), P("groups")),
        check_vma=False,
    )
```

```python
import functools

import jax
import jax.numpy as jnp
from jax import lax
from jax.experimental import pallas as pl
from jax.experimental.pallas import tpu as pltpu
from jax.sharding import PartitionSpec as P

CAP = 4
RING = ("row", "col")
SMEM = pl.BlockSpec(memory_space=pltpu.SMEM)
VMEM = pl.BlockSpec(memory_space=pltpu.VMEM)
HBM = pl.BlockSpec(memory_space=pltpu.HBM)
MIB = 1024 * 1024


def permute(value, pairs):
    return lax.ppermute(value, RING, pairs)


def ring_steps():
    n, cols = lax.axis_size(RING), lax.axis_size("col")
    if n & (n - 1) or cols & (cols - 1) or cols < 4:
        return None
    return [1] + [cols << k for k in range((n // cols).bit_length() - 1)] + [2 << k for k in range(cols.bit_length() - 2)]


def partner(value, step):
    return permute(value, [(i, i ^ step) for i in range(lax.axis_size(RING))])


def rank(bits, rows, order, first):
    count = 0
    for r in range(rows):
        named = lax.rem(lax.shift_right_logical(bits, r), 2)
        order[first + jnp.where(named > 0, jnp.minimum(count, CAP), CAP)] = r
        count = count + named


def clear(ref, count, value):
    for q in range(count):
        ref[q] = value


def copy_in(source, target, sem):
    copy = pltpu.make_async_copy(source, target, sem)
    copy.start()
    return copy


def spread_kernel(total_rows, cols_hbm, keep_hbm, flag, x_hbm, own, outer, inner, table, meta,
                  cols, keep, x, slots_of, order, sem):
    rows, slots = cols.shape
    block = x.shape[-1]
    wide = 3 * rows
    across = rows + 2 * CAP
    lists = [copy_in(cols_hbm, cols, sem.at[0]), copy_in(keep_hbm, keep, sem.at[1])]
    blocks = [copy_in(x_hbm.at[i], x.at[i], sem.at[2 + i]) for i in range(rows)]
    clear(slots_of, rows * wide, -1)
    for copy in lists:
        copy.wait()
    base = cols[0, 0]
    odd = lax.rem(lax.div(base, rows), 2)
    ahead = jnp.where(odd == 1, 0, rows)
    behind = jnp.where(odd == 1, 2 * rows, rows) - (total_rows - rows)
    bits = 0
    for i in range(rows):
        for s in range(slots):
            rel = cols[i, s] - base
            rel = jnp.where(rel < 0, rel + total_rows, rel)
            rel = rel + jnp.where(rel >= 2 * rows, behind, jnp.where(rel >= rows, ahead, 0))
            slots_of[i * wide + rel] = 2 * s + keep[i, s]
            bits = bits | lax.shift_left(1, rel)
    rank(lax.shift_right_logical(bits, rows), rows, order, 0)
    rank(lax.shift_right_logical(bits, 2 * rows), rows, order, CAP + 1)
    for c in range(2 * CAP):
        meta[c] = order[c + c // CAP]
    meta[2 * CAP] = base
    meta[2 * CAP + 1] = flag[0]
    for i in range(rows):
        span = pl.ds(i * block, block)
        blocks[i].wait()
        for k in range(rows):
            code = slots_of[i * wide + k]
            table[i * across + k] = code
            own[span, pl.ds(k * block, block)] = x[i, lax.shift_right_logical(code, 1)]
        for first, target, start, shift in ((0, outer, rows, 0), (CAP + 1, inner, 2 * rows, CAP)):
            for c in range(CAP):
                code = slots_of[i * wide + start + order[first + c]]
                table[i * across + rows + shift + c] = code
                value = x[i, lax.shift_right_logical(jnp.maximum(code, 0), 1)]
                target[span, pl.ds(c * block, block)] = jnp.where(code >= 0, value, jnp.zeros_like(value))


def pack_kernel(meta, cols_outer, own, outer, far_out, near_out, asked, order):
    rows, slots = cols_outer.shape
    block = own.shape[0] // rows
    base = meta[2 * CAP]
    bits = 0
    for i in range(rows):
        for s in range(slots):
            rel = cols_outer[i, s] - base
            bits = bits | lax.shift_left(1, jnp.where((rel >= 0) & (rel < rows), rel, rows))
    rank(bits, rows, order, 0)
    for a in range(CAP):
        asked[a] = order[a]
        span = pl.ds(a * block, block)
        row = pl.ds(pl.multiple_of(order[a] * block, block), block)
        far_out[span, :] = outer[row, :]
        for b in range(CAP):
            column = pl.ds(pl.multiple_of(order[b] * block, block), block)
            near_out[span, pl.ds(b * block, block)] = own[row, column]
    count = 0
    for r in range(rows):
        left = 1 - lax.rem(lax.shift_right_logical(bits, r), 2)
        asked[CAP + jnp.where(left > 0, jnp.minimum(count, rows - CAP), rows - CAP)] = r
        count = count + left


def signs(meta):
    on = meta[2 * CAP + 1] == 1
    return jnp.where(on, 0.0, 2.0), jnp.where(on, 1.0, -1.0)


def diagonal(square):
    n = square.shape[-1]
    on = lax.broadcasted_iota(jnp.int32, (n, n), 0) == lax.broadcasted_iota(jnp.int32, (n, n), 1)
    return jnp.sum(jnp.where(on, square, 0.0))


def kept(code):
    return lax.rem(jnp.maximum(code, 0), 2).astype(jnp.float32)


def give(stage, out, i, code, sem):
    copy = pltpu.make_async_copy(stage, out.at[i, lax.shift_right_logical(jnp.maximum(code, 0), 1)], sem)

    @pl.when(code >= 0)
    def _():
        copy.start()

    def wait():
        @pl.when(code >= 0)
        def _():
            copy.wait()
    return wait


def own_kernel(table, meta, asked, cols_inner, own, outer, inner, x_inner, out, base_far, base_near, turned, trace,
               got_own, got_far, square, side, stage, slots_of, order, sem, sem_got):
    rows, slots = cols_inner.shape
    block = own.shape[0] // rows
    across = rows + 2 * CAP
    twice, sign = signs(meta)
    left = own[...]
    left_signed = left * sign.astype(left.dtype)
    inner_signed = inner[...] * sign.astype(left.dtype)
    wide = 2 * rows + 1
    clear(slots_of, rows * wide, -1)
    mine, theirs = meta[2 * CAP], cols_inner[0, 0]
    bits = 0
    for i in range(rows):
        for s in range(slots):
            near = cols_inner[i, s] - theirs
            far = cols_inner[i, s] - mine
            far = jnp.where((far >= 0) & (far < rows), far, rows)
            bits = bits | lax.shift_left(1, far)
            slots_of[i * wide + jnp.where((near >= 0) & (near < rows), near, rows + far)] = s
    rank(bits, rows, order, 0)
    arrive = []
    for r in range(CAP):
        row = meta[CAP + r]
        span = pl.ds(r * block, block)
        for c in range(CAP):
            place = pl.ds(c * block, block)
            slot = slots_of[row * wide + meta[CAP + c]]
            arrive.append(copy_in(x_inner.at[row, jnp.maximum(slot, 0)], got_own.at[span, place], sem_got))
            slot = slots_of[row * wide + rows + order[c]]
            far_slot = jnp.maximum(slot, 0)
            arrive.append(copy_in(x_inner.at[row, far_slot], got_far.at[span, place], sem_got))
    base_near[...] = (twice * outer[...].astype(jnp.float32)
                      + jnp.dot(left_signed, outer[...], preferred_element_type=jnp.float32))
    square[...] = twice * left.astype(jnp.float32) + jnp.dot(left_signed, left, preferred_element_type=jnp.float32)
    for r in range(CAP):
        for c in range(CAP):
            value = outer[pl.ds(pl.multiple_of(asked[c] * block, block), block), pl.ds(r * block, block)]
            turned[pl.ds(r * block, block), pl.ds(c * block, block)] = value.T
    for copy in arrive:
        copy.wait()
    for r in range(CAP):
        for c in range(CAP):
            @pl.when(slots_of[meta[CAP + r] * wide + rows + order[c]] < 0)
            def _():
                got_far[pl.ds(r * block, block), pl.ds(c * block, block)] = jnp.zeros((block, block), got_far.dtype)
    part = jnp.dot(inner_signed, got_far[...], preferred_element_type=jnp.float32)
    for c in range(CAP):
        place = pl.ds(pl.multiple_of(order[c] * block, block), block)
        square[:, place] = square[:, place] + part[:, c * block:(c + 1) * block]
    for c in range(CAP):
        place = pl.ds(pl.multiple_of(asked[c] * block, block), block)
        base_far[:, pl.ds(c * block, block)] = square[:, place]
    total = jnp.zeros((block, block), jnp.float32)
    for i in range(rows):
        span = pl.ds(i * block, block)
        total = total + kept(table[i * across + i]) * square[span, span]
    trace[0] = diagonal(total)
    side[...] = twice * inner[...].astype(jnp.float32) + jnp.dot(
        jnp.concatenate([left_signed, inner_signed], axis=1), jnp.concatenate([inner[...], got_own[...]], axis=0),
        preferred_element_type=jnp.float32)
    waits = []
    for i in range(rows):
        span = pl.ds(i * block, block)
        for e in range(rows - CAP):
            k = asked[CAP + e]
            code = table[i * across + k]
            value = square[span, pl.ds(pl.multiple_of(k * block, block), block)]
            stage[i, CAP + e] = (kept(code) * value).astype(stage.dtype)
            waits.append(give(stage.at[i, CAP + e], out, i, code, sem))
        for c in range(CAP):
            code = table[i * across + rows + CAP + c]
            stage[i, c] = (kept(code) * side[span, pl.ds(c * block, block)]).astype(stage.dtype)
            waits.append(give(stage.at[i, c], out, i, code, sem))
    for wait in waits:
        wait()


def trace_kernel(rows, table, meta, asked, turned, far, trace_own, trace):
    block = turned.shape[0] // CAP
    across = rows + 2 * CAP
    total = jnp.zeros((8, block), jnp.float32)
    for c in range(CAP):
        mine = asked[c]
        column = pl.ds(c * block, block)
        part = far[:, column].astype(jnp.float32) * turned[:, column].astype(jnp.float32)
        total = total + kept(table[mine * across + mine]) * jnp.sum(part.reshape(CAP * block // 8, 8, block), axis=0)
    value = (trace_own[0] + signs(meta)[1] * jnp.sum(total)) * (1.0 / total_count(rows, block))
    trace[...] = jnp.full(trace.shape, value, jnp.float32)


def total_count(rows, block):
    return rows * block * lax.axis_size(RING)


def finish_half(near, rows, table, meta, asked, outer, base, got, out, stage, sem):
    block = outer.shape[0] // rows
    across = rows + 2 * CAP
    right = got[...] * signs(meta)[1].astype(got.dtype)
    waits = []
    chunk = rows // 2
    for first in range(0, rows, chunk):
        tall = pl.ds(first * block, chunk * block)
        value = base[tall, :] + jnp.dot(outer[tall, :], right, preferred_element_type=jnp.float32)
        codes = {}
        for i in range(first, first + chunk):
            low = (i - first) * block
            for c in range(CAP):
                code = table[i * across + (rows + c if near else asked[c])]
                codes[i, c] = code
                stage[i, c] = (kept(code) * value[low:low + block, c * block:(c + 1) * block]).astype(stage.dtype)
        for (i, c), code in codes.items():
            waits.append(give(stage.at[i, c], out, i, code, sem))
    for wait in waits:
        wait()


def far_kernel(rows, table, meta, asked, outer, base, far, _, out, *scratch):
    finish_half(False, rows, table, meta, asked, outer, base, far, out, *scratch)


def last_kernel(rows, table, meta, asked, outer, base, near, _, out, *scratch):
    finish_half(True, rows, table, meta, asked, outer, base, near, out, *scratch)


def body(x, cols, keep, flag):
    rows, slots, block = x.shape[0], x.shape[1], x.shape[2]
    n = lax.axis_size(RING)
    total_rows = rows * n
    bf16, f32, i32 = x.dtype, jnp.float32, jnp.int32
    wide, narrow, across = rows * block, CAP * block, rows + 2 * CAP
    dma = pltpu.SemaphoreType.DMA

    def ints(*shape):
        return pltpu.SMEM(shape, i32)

    def call(kernel, outs, in_specs, scratch, mib, aliases=None, first=None):
        def run(*refs):
            kernel(*(() if first is None else (first,)), *refs)
        return pl.pallas_call(
            run, out_shape=[(pltpu.HBM if len(o) > 3 else jax.ShapeDtypeStruct)(*o[:2]) for o in outs], in_specs=in_specs,
            out_specs=[o[2] for o in outs], scratch_shapes=scratch, name=kernel.__name__,
            input_output_aliases=aliases or {},
            cost_estimate=pl.CostEstimate(flops=1, bytes_accessed=1, transcendentals=0),
            compiler_params=pltpu.CompilerParams(vmem_limit_bytes=mib * MIB))

    inside = [(i, i ^ 1) for i in range(n)]
    upward = [(i, (i + 1) % n) for i in range(1, n, 2)]
    outside = upward + [(b, a) for a, b in upward]
    hbm = functools.partial(pltpu.with_memory_space_constraint, memory_space=pltpu.HBM)
    barrier = lax.optimization_barrier

    x_inner = permute(x, inside)
    cols_inner = permute(cols, inside)
    cols_outer = permute(cols, outside)
    own, outer, inner, table, meta = call(
        spread_kernel,
        [((wide, wide), bf16, VMEM), ((wide, narrow), bf16, VMEM), ((wide, narrow), bf16, VMEM),
         ((rows * across,), i32, SMEM), ((2 * CAP + 2,), i32, SMEM)],
        [HBM] * 2 + [SMEM, HBM], [ints(rows, slots), ints(rows, slots), pltpu.VMEM(x.shape, bf16), ints(rows * 3 * rows),
                    ints(2 * (CAP + 1)), dma((2 + rows,))], 16, first=total_rows)(hbm(cols), hbm(keep), flag, hbm(x))
    far_out, near_out, asked = call(
        pack_kernel,
        [((narrow, narrow), bf16, VMEM), ((narrow, narrow), bf16, VMEM), ((CAP + rows - CAP + 1,), i32, SMEM)],
        [SMEM] * 2 + [VMEM] * 2, [ints(CAP + 1)], 16,
    )(meta, cols_outer, own, outer)
    far = permute(far_out, outside)
    out, base_far, base_near, turned, trace_own = call(
        own_kernel,
        [(x.shape, bf16, HBM), ((wide, narrow), f32, VMEM), ((wide, narrow), f32, VMEM),
         ((narrow, narrow), bf16, VMEM), ((1,), f32, SMEM)],
        [SMEM] * 4 + [VMEM] * 3 + [HBM],
        [pltpu.VMEM((narrow, narrow), bf16), pltpu.VMEM((narrow, narrow), bf16), pltpu.VMEM((wide, wide), f32),
         pltpu.VMEM((wide, narrow), f32), pltpu.VMEM((rows, rows, block, block), bf16), ints(rows * (2 * rows + 1)),
         ints(CAP + 1), dma, dma], 24)(table, meta, asked, cols_inner, own, outer, inner, x_inner)
    partial, = call(
        trace_kernel, [((8, block), f32, VMEM)], [SMEM] * 3 + [VMEM, VMEM, SMEM],
        [], 12, first=rows)(table, meta, asked, turned, far, trace_own)
    near_out, partial = barrier((near_out, partial))
    near = permute(near_out, outside)
    half_scratch = [pltpu.VMEM((rows, CAP, block, block), bf16), dma]

    def half(kernel, base, got, out):
        result, = call(
            kernel, [(x.shape, bf16, HBM)], [SMEM] * 3 + [VMEM] * 3 + [HBM], half_scratch, 16, {6: 0}, first=rows,
        )(table, meta, asked, outer, base, got, out)
        return result

    steps = ring_steps()
    if steps is None:
        total = lax.psum(partial, RING)
        return half(last_kernel, base_near, near, half(far_kernel, base_far, far, out)), total[0, :1]
    partial = partial + partner(partial, steps[0])
    out, partial = barrier((out, partial))
    out = half(far_kernel, base_far, far, out)
    out, partial = barrier((out, partial))
    for step in steps[1:-1]:
        partial = partial + partner(partial, step)
    ready, partial = barrier((out, partial))
    out = half(last_kernel, base_near, near, ready)
    other, out = barrier((partner(partial, steps[-1] | 1), out))
    return out, (partial + other)[0, :1]


def solution(mesh):
    placed = (
        P(("groups", "row", "col"), None, None, None),
        P(("groups", "row", "col"), None),
        P(("groups", "row", "col"), None),
        P("groups"),
    )
    return jax.shard_map(
        body,
        mesh=mesh,
        in_specs=placed,
        out_specs=(P(("groups", "row", "col"), None, None, None), P("groups")),
        check_vma=False,
    )
```

```python
import functools

import jax
import jax.numpy as jnp
from jax import lax
from jax.experimental import pallas as pl
from jax.experimental.pallas import tpu as pltpu
from jax.sharding import PartitionSpec as P

CAP = 4
RING = ("row", "col")
SMEM = pl.BlockSpec(memory_space=pltpu.SMEM)
VMEM = pl.BlockSpec(memory_space=pltpu.VMEM)
HBM = pl.BlockSpec(memory_space=pltpu.HBM)
MIB = 1024 * 1024


def permute(value, pairs):
    return lax.ppermute(value, RING, pairs)


def ring_steps():
    n, cols = lax.axis_size(RING), lax.axis_size("col")
    if n & (n - 1) or cols & (cols - 1) or cols < 4:
        return None
    return [1] + [cols << k for k in range((n // cols).bit_length() - 1)] + [2 << k for k in range(cols.bit_length() - 2)]


def partner(value, step):
    return permute(value, [(i, i ^ step) for i in range(lax.axis_size(RING))])


def rank(bits, rows, order, first):
    count = 0
    for r in range(rows):
        named = lax.rem(lax.shift_right_logical(bits, r), 2)
        order[first + jnp.where(named > 0, jnp.minimum(count, CAP), CAP)] = r
        count = count + named


def clear(ref, count, value):
    for q in range(count):
        ref[q] = value


def copy_in(source, target, sem):
    copy = pltpu.make_async_copy(source, target, sem)
    copy.start()
    return copy


def spread_kernel(total_rows, cols_hbm, keep_hbm, flag, x_hbm, own, outer, inner, table, meta,
                  cols, keep, x, slots_of, order, sem):
    rows, slots = cols.shape
    block = x.shape[-1]
    wide = 3 * rows
    across = rows + 2 * CAP
    lists = [copy_in(cols_hbm, cols, sem.at[0]), copy_in(keep_hbm, keep, sem.at[1])]
    blocks = [copy_in(x_hbm.at[i], x.at[i], sem.at[2 + i]) for i in range(rows)]
    clear(slots_of, rows * wide, -1)
    for copy in lists:
        copy.wait()
    base = cols[0, 0]
    odd = lax.rem(lax.div(base, rows), 2)
    ahead = jnp.where(odd == 1, 0, rows)
    behind = jnp.where(odd == 1, 2 * rows, rows) - (total_rows - rows)
    bits = 0
    for i in range(rows):
        for s in range(slots):
            rel = cols[i, s] - base
            rel = jnp.where(rel < 0, rel + total_rows, rel)
            rel = rel + jnp.where(rel >= 2 * rows, behind, jnp.where(rel >= rows, ahead, 0))
            slots_of[i * wide + rel] = 2 * s + keep[i, s]
            bits = bits | lax.shift_left(1, rel)
    rank(lax.shift_right_logical(bits, rows), rows, order, 0)
    rank(lax.shift_right_logical(bits, 2 * rows), rows, order, CAP + 1)
    for c in range(2 * CAP):
        meta[c] = order[c + c // CAP]
    meta[2 * CAP] = base
    meta[2 * CAP + 1] = flag[0]
    for i in range(rows):
        span = pl.ds(i * block, block)
        blocks[i].wait()
        for k in range(rows):
            code = slots_of[i * wide + k]
            table[i * across + k] = code
            own[span, pl.ds(k * block, block)] = x[i, lax.shift_right_logical(code, 1)]
        for first, target, start, shift in ((0, outer, rows, 0), (CAP + 1, inner, 2 * rows, CAP)):
            for c in range(CAP):
                code = slots_of[i * wide + start + order[first + c]]
                table[i * across + rows + shift + c] = code
                value = x[i, lax.shift_right_logical(jnp.maximum(code, 0), 1)]
                target[span, pl.ds(c * block, block)] = jnp.where(code >= 0, value, jnp.zeros_like(value))


def pack_kernel(meta, cols_outer, own, outer, far_out, near_out, asked, order):
    rows, slots = cols_outer.shape
    block = own.shape[0] // rows
    base = meta[2 * CAP]
    bits = 0
    for i in range(rows):
        for s in range(slots):
            rel = cols_outer[i, s] - base
            bits = bits | lax.shift_left(1, jnp.where((rel >= 0) & (rel < rows), rel, rows))
    rank(bits, rows, order, 0)
    for a in range(CAP):
        asked[a] = order[a]
        span = pl.ds(a * block, block)
        row = pl.ds(pl.multiple_of(order[a] * block, block), block)
        far_out[span, :] = outer[row, :]
        for b in range(CAP):
            column = pl.ds(pl.multiple_of(order[b] * block, block), block)
            near_out[span, pl.ds(b * block, block)] = own[row, column]
    count = 0
    for r in range(rows):
        left = 1 - lax.rem(lax.shift_right_logical(bits, r), 2)
        asked[CAP + jnp.where(left > 0, jnp.minimum(count, rows - CAP), rows - CAP)] = r
        count = count + left


def signs(meta):
    on = meta[2 * CAP + 1] == 1
    return jnp.where(on, 0.0, 2.0), jnp.where(on, 1.0, -1.0)


def diagonal(square):
    n = square.shape[-1]
    on = lax.broadcasted_iota(jnp.int32, (n, n), 0) == lax.broadcasted_iota(jnp.int32, (n, n), 1)
    return jnp.sum(jnp.where(on, square, 0.0))


def kept(code):
    return lax.rem(jnp.maximum(code, 0), 2).astype(jnp.float32)


def give(stage, out, i, code, sem):
    copy = pltpu.make_async_copy(stage, out.at[i, lax.shift_right_logical(jnp.maximum(code, 0), 1)], sem)

    @pl.when(code >= 0)
    def _():
        copy.start()

    def wait():
        @pl.when(code >= 0)
        def _():
            copy.wait()
    return wait


def own_kernel(table, meta, asked, cols_inner, own, outer, inner, x_inner, out, base_far, base_near, turned, trace,
               got_own, got_far, square, side, stage, slots_of, order, sem, sem_got):
    rows, slots = cols_inner.shape
    block = own.shape[0] // rows
    across = rows + 2 * CAP
    twice, sign = signs(meta)
    left = own[...]
    left_signed = left * sign.astype(left.dtype)
    inner_signed = inner[...] * sign.astype(left.dtype)
    wide = 2 * rows + 1
    clear(slots_of, rows * wide, -1)
    mine, theirs = meta[2 * CAP], cols_inner[0, 0]
    bits = 0
    for i in range(rows):
        for s in range(slots):
            near = cols_inner[i, s] - theirs
            far = cols_inner[i, s] - mine
            far = jnp.where((far >= 0) & (far < rows), far, rows)
            bits = bits | lax.shift_left(1, far)
            slots_of[i * wide + jnp.where((near >= 0) & (near < rows), near, rows + far)] = s
    rank(bits, rows, order, 0)
    arrive = []
    for r in range(CAP):
        row = meta[CAP + r]
        span = pl.ds(r * block, block)
        for c in range(CAP):
            place = pl.ds(c * block, block)
            slot = slots_of[row * wide + meta[CAP + c]]
            arrive.append(copy_in(x_inner.at[row, jnp.maximum(slot, 0)], got_own.at[span, place], sem_got))
            slot = slots_of[row * wide + rows + order[c]]
            far_slot = jnp.maximum(slot, 0)
            arrive.append(copy_in(x_inner.at[row, far_slot], got_far.at[span, place], sem_got))
    base_near[...] = (twice * outer[...].astype(jnp.float32)
                      + jnp.dot(left_signed, outer[...], preferred_element_type=jnp.float32))
    square[...] = twice * left.astype(jnp.float32) + jnp.dot(left_signed, left, preferred_element_type=jnp.float32)
    for r in range(CAP):
        for c in range(CAP):
            value = outer[pl.ds(pl.multiple_of(asked[c] * block, block), block), pl.ds(r * block, block)]
            weight = sign * kept(table[asked[c] * across + asked[c]])
            turned[pl.ds(r * block, block), pl.ds(c * block, block)] = (value * weight.astype(value.dtype)).T
    for copy in arrive:
        copy.wait()
    for r in range(CAP):
        for c in range(CAP):
            @pl.when(slots_of[meta[CAP + r] * wide + rows + order[c]] < 0)
            def _():
                got_far[pl.ds(r * block, block), pl.ds(c * block, block)] = jnp.zeros((block, block), got_far.dtype)
    part = jnp.dot(inner_signed, got_far[...], preferred_element_type=jnp.float32)
    for c in range(CAP):
        place = pl.ds(pl.multiple_of(order[c] * block, block), block)
        square[:, place] = square[:, place] + part[:, c * block:(c + 1) * block]
    for c in range(CAP):
        place = pl.ds(pl.multiple_of(asked[c] * block, block), block)
        base_far[:, pl.ds(c * block, block)] = square[:, place]
    total = jnp.zeros((block, block), jnp.float32)
    for i in range(rows):
        span = pl.ds(i * block, block)
        total = total + kept(table[i * across + i]) * square[span, span]
    trace[0] = diagonal(total)
    side[...] = twice * inner[...].astype(jnp.float32) + jnp.dot(
        jnp.concatenate([left_signed, inner_signed], axis=1), jnp.concatenate([inner[...], got_own[...]], axis=0),
        preferred_element_type=jnp.float32)
    waits = []
    for i in range(rows):
        span = pl.ds(i * block, block)
        for e in range(rows - CAP):
            k = asked[CAP + e]
            code = table[i * across + k]
            value = square[span, pl.ds(pl.multiple_of(k * block, block), block)]
            stage[i, CAP + e] = (kept(code) * value).astype(stage.dtype)
            waits.append(give(stage.at[i, CAP + e], out, i, code, sem))
        for c in range(CAP):
            code = table[i * across + rows + CAP + c]
            stage[i, c] = (kept(code) * side[span, pl.ds(c * block, block)]).astype(stage.dtype)
            waits.append(give(stage.at[i, c], out, i, code, sem))
    for wait in waits:
        wait()


def trace_kernel(rows, turned, far, trace_own, trace):
    tall, block = turned.shape[0], turned.shape[0] // CAP
    part = far[...].astype(jnp.float32) * turned[...].astype(jnp.float32)
    value = trace_own[0] + jnp.sum(jnp.sum(part.reshape(tall // 8, 8, tall), axis=0))
    trace[...] = jnp.full(trace.shape, value * (1.0 / total_count(rows, block)), jnp.float32)


def total_count(rows, block):
    return rows * block * lax.axis_size(RING)


def finish_half(near, rows, table, meta, asked, outer, base, got, out, stage, sem):
    block = outer.shape[0] // rows
    across = rows + 2 * CAP
    right = got[...] * signs(meta)[1].astype(got.dtype)
    waits = []
    chunk = rows // 2
    for first in range(0, rows, chunk):
        tall = pl.ds(first * block, chunk * block)
        value = base[tall, :] + jnp.dot(outer[tall, :], right, preferred_element_type=jnp.float32)
        codes = {}
        for i in range(first, first + chunk):
            low = (i - first) * block
            for c in range(CAP):
                code = table[i * across + (rows + c if near else asked[c])]
                codes[i, c] = code
                stage[i, c] = (kept(code) * value[low:low + block, c * block:(c + 1) * block]).astype(stage.dtype)
        for (i, c), code in codes.items():
            waits.append(give(stage.at[i, c], out, i, code, sem))
    for wait in waits:
        wait()


def far_kernel(rows, table, meta, asked, outer, base, far, _, out, *scratch):
    finish_half(False, rows, table, meta, asked, outer, base, far, out, *scratch)


def last_kernel(rows, table, meta, asked, outer, base, near, _, out, *scratch):
    finish_half(True, rows, table, meta, asked, outer, base, near, out, *scratch)


def body(x, cols, keep, flag):
    rows, slots, block = x.shape[0], x.shape[1], x.shape[2]
    n = lax.axis_size(RING)
    total_rows = rows * n
    bf16, f32, i32 = x.dtype, jnp.float32, jnp.int32
    wide, narrow, across = rows * block, CAP * block, rows + 2 * CAP
    dma = pltpu.SemaphoreType.DMA

    def ints(*shape):
        return pltpu.SMEM(shape, i32)

    def call(kernel, outs, in_specs, scratch, mib, aliases=None, first=None):
        def run(*refs):
            kernel(*(() if first is None else (first,)), *refs)
        return pl.pallas_call(
            run, out_shape=[(pltpu.HBM if len(o) > 3 else jax.ShapeDtypeStruct)(*o[:2]) for o in outs], in_specs=in_specs,
            out_specs=[o[2] for o in outs], scratch_shapes=scratch, name=kernel.__name__,
            input_output_aliases=aliases or {},
            cost_estimate=pl.CostEstimate(flops=1, bytes_accessed=1, transcendentals=0),
            compiler_params=pltpu.CompilerParams(vmem_limit_bytes=mib * MIB))

    inside = [(i, i ^ 1) for i in range(n)]
    upward = [(i, (i + 1) % n) for i in range(1, n, 2)]
    outside = upward + [(b, a) for a, b in upward]
    hbm = functools.partial(pltpu.with_memory_space_constraint, memory_space=pltpu.HBM)
    barrier = lax.optimization_barrier

    x_inner = permute(x, inside)
    cols_inner = permute(cols, inside)
    cols_outer = permute(cols, outside)
    own, outer, inner, table, meta = call(
        spread_kernel,
        [((wide, wide), bf16, VMEM), ((wide, narrow), bf16, VMEM), ((wide, narrow), bf16, VMEM),
         ((rows * across,), i32, SMEM), ((2 * CAP + 2,), i32, SMEM)],
        [HBM] * 2 + [SMEM, HBM], [ints(rows, slots), ints(rows, slots), pltpu.VMEM(x.shape, bf16), ints(rows * 3 * rows),
                    ints(2 * (CAP + 1)), dma((2 + rows,))], 16, first=total_rows)(hbm(cols), hbm(keep), flag, hbm(x))
    far_out, near_out, asked = call(
        pack_kernel,
        [((narrow, narrow), bf16, VMEM), ((narrow, narrow), bf16, VMEM), ((CAP + rows - CAP + 1,), i32, SMEM)],
        [SMEM] * 2 + [VMEM] * 2, [ints(CAP + 1)], 16,
    )(meta, cols_outer, own, outer)
    far = permute(far_out, outside)
    out, base_far, base_near, turned, trace_own = call(
        own_kernel,
        [(x.shape, bf16, HBM), ((wide, narrow), f32, VMEM), ((wide, narrow), f32, VMEM),
         ((narrow, narrow), bf16, VMEM), ((1,), f32, SMEM)],
        [SMEM] * 4 + [VMEM] * 3 + [HBM],
        [pltpu.VMEM((narrow, narrow), bf16), pltpu.VMEM((narrow, narrow), bf16), pltpu.VMEM((wide, wide), f32),
         pltpu.VMEM((wide, narrow), f32), pltpu.VMEM((rows, rows, block, block), bf16), ints(rows * (2 * rows + 1)),
         ints(CAP + 1), dma, dma], 24)(table, meta, asked, cols_inner, own, outer, inner, x_inner)
    partial, = call(
        trace_kernel, [((8, block), f32, VMEM)], [VMEM, VMEM, SMEM], [], 12, first=rows)(turned, far, trace_own)
    near_out, partial = barrier((near_out, partial))
    near = permute(near_out, outside)
    half_scratch = [pltpu.VMEM((rows, CAP, block, block), bf16), dma]

    def half(kernel, base, got, out):
        result, = call(
            kernel, [(x.shape, bf16, HBM)], [SMEM] * 3 + [VMEM] * 3 + [HBM], half_scratch, 16, {6: 0}, first=rows,
        )(table, meta, asked, outer, base, got, out)
        return result

    steps = ring_steps()
    if steps is None:
        total = lax.psum(partial, RING)
        return half(last_kernel, base_near, near, half(far_kernel, base_far, far, out)), total[0, :1]
    partial = partial + partner(partial, steps[0])
    out, partial = barrier((out, partial))
    out = half(far_kernel, base_far, far, out)
    out, partial = barrier((out, partial))
    for step in steps[1:-1]:
        partial = partial + partner(partial, step)
    ready, partial = barrier((out, partial))
    out = half(last_kernel, base_near, near, ready)
    other, out = barrier((partner(partial, steps[-1] | 1), out))
    return out, (partial + other)[0, :1]


def solution(mesh):
    placed = (
        P(("groups", "row", "col"), None, None, None),
        P(("groups", "row", "col"), None),
        P(("groups", "row", "col"), None),
        P("groups"),
    )
    return jax.shard_map(
        body,
        mesh=mesh,
        in_specs=placed,
        out_specs=(P(("groups", "row", "col"), None, None, None), P("groups")),
        check_vma=False,
    )
```

```python
import functools

import jax
import jax.numpy as jnp
from jax import lax
from jax.experimental import pallas as pl
from jax.experimental.pallas import tpu as pltpu
from jax.sharding import PartitionSpec as P

CAP = 4
RING = ("row", "col")
SMEM = pl.BlockSpec(memory_space=pltpu.SMEM)
VMEM = pl.BlockSpec(memory_space=pltpu.VMEM)
HBM = pl.BlockSpec(memory_space=pltpu.HBM)
MIB = 1024 * 1024


def permute(value, pairs):
    return lax.ppermute(value, RING, pairs)


def ring_steps():
    n, cols = lax.axis_size(RING), lax.axis_size("col")
    if n & (n - 1) or cols & (cols - 1) or cols < 4:
        return None
    return [1] + [cols << k for k in range((n // cols).bit_length() - 1)] + [2 << k for k in range(cols.bit_length() - 2)]


def partner(value, step):
    return permute(value, [(i, i ^ step) for i in range(lax.axis_size(RING))])


def rank(bits, rows, order, first):
    count = 0
    for r in range(rows):
        named = lax.rem(lax.shift_right_logical(bits, r), 2)
        order[first + jnp.where(named > 0, jnp.minimum(count, CAP), CAP)] = r
        count = count + named


def clear(ref, count, value):
    for q in range(count):
        ref[q] = value


def copy_in(source, target, sem):
    copy = pltpu.make_async_copy(source, target, sem)
    copy.start()
    return copy


def spread_kernel(total_rows, cols_hbm, keep_hbm, flag, x_hbm, own, outer, inner, table, meta,
                  cols, keep, x, slots_of, order, sem):
    rows, slots = cols.shape
    block = x.shape[-1]
    wide = 3 * rows
    across = rows + 2 * CAP
    lists = [copy_in(cols_hbm, cols, sem.at[0]), copy_in(keep_hbm, keep, sem.at[1])]
    blocks = [copy_in(x_hbm.at[i], x.at[i], sem.at[2 + i]) for i in range(rows)]
    clear(slots_of, rows * wide, -1)
    for copy in lists:
        copy.wait()
    base = cols[0, 0]
    odd = lax.rem(lax.div(base, rows), 2)
    ahead = jnp.where(odd == 1, 0, rows)
    behind = jnp.where(odd == 1, 2 * rows, rows) - (total_rows - rows)
    bits = 0
    for i in range(rows):
        for s in range(slots):
            rel = cols[i, s] - base
            rel = jnp.where(rel < 0, rel + total_rows, rel)
            rel = rel + jnp.where(rel >= 2 * rows, behind, jnp.where(rel >= rows, ahead, 0))
            slots_of[i * wide + rel] = 2 * s + keep[i, s]
            bits = bits | lax.shift_left(1, rel)
    rank(lax.shift_right_logical(bits, rows), rows, order, 0)
    rank(lax.shift_right_logical(bits, 2 * rows), rows, order, CAP + 1)
    for c in range(2 * CAP):
        meta[c] = order[c + c // CAP]
    meta[2 * CAP] = base
    meta[2 * CAP + 1] = flag[0]
    table[rows * across] = flag[0]
    for i in range(rows):
        span = pl.ds(i * block, block)
        blocks[i].wait()
        for k in range(rows):
            code = slots_of[i * wide + k]
            table[i * across + k] = code
            own[span, pl.ds(k * block, block)] = x[i, lax.shift_right_logical(code, 1)]
        for first, target, start, shift in ((0, outer, rows, 0), (CAP + 1, inner, 2 * rows, CAP)):
            for c in range(CAP):
                code = slots_of[i * wide + start + order[first + c]]
                table[i * across + rows + shift + c] = code
                value = x[i, lax.shift_right_logical(jnp.maximum(code, 0), 1)]
                target[span, pl.ds(c * block, block)] = jnp.where(code >= 0, value, jnp.zeros_like(value))


def pack_kernel(meta, cols_outer, own, outer, far_out, near_out, asked, order):
    rows, slots = cols_outer.shape
    block = own.shape[0] // rows
    base = meta[2 * CAP]
    bits = 0
    for i in range(rows):
        for s in range(slots):
            rel = cols_outer[i, s] - base
            bits = bits | lax.shift_left(1, jnp.where((rel >= 0) & (rel < rows), rel, rows))
    rank(bits, rows, order, 0)
    for a in range(CAP):
        asked[a] = order[a]
        span = pl.ds(a * block, block)
        row = pl.ds(pl.multiple_of(order[a] * block, block), block)
        far_out[span, :] = outer[row, :]
        for b in range(CAP):
            column = pl.ds(pl.multiple_of(order[b] * block, block), block)
            near_out[span, pl.ds(b * block, block)] = own[row, column]
    count = 0
    for r in range(rows):
        left = 1 - lax.rem(lax.shift_right_logical(bits, r), 2)
        asked[CAP + jnp.where(left > 0, jnp.minimum(count, rows - CAP), rows - CAP)] = r
        count = count + left


def signs(meta):
    on = meta[2 * CAP + 1] == 1
    return jnp.where(on, 0.0, 2.0), jnp.where(on, 1.0, -1.0)


def diagonal(square):
    n = square.shape[-1]
    on = lax.broadcasted_iota(jnp.int32, (n, n), 0) == lax.broadcasted_iota(jnp.int32, (n, n), 1)
    return jnp.sum(jnp.where(on, square, 0.0))


def kept(code):
    return lax.rem(jnp.maximum(code, 0), 2).astype(jnp.float32)


def give(stage, out, i, code, sem):
    copy = pltpu.make_async_copy(stage, out.at[i, lax.shift_right_logical(jnp.maximum(code, 0), 1)], sem)

    @pl.when(code >= 0)
    def _():
        copy.start()

    def wait():
        @pl.when(code >= 0)
        def _():
            copy.wait()
    return wait


def own_kernel(table, meta, asked, cols_inner, own, outer, inner, x_inner, out, base_far, base_near, turned, trace,
               got_own, got_far, square, side, stage, slots_of, order, sem, sem_got):
    rows, slots = cols_inner.shape
    block = own.shape[0] // rows
    across = rows + 2 * CAP
    twice, sign = signs(meta)
    left = own[...]
    left_signed = left * sign.astype(left.dtype)
    inner_signed = inner[...] * sign.astype(left.dtype)
    wide = 2 * rows + 1
    clear(slots_of, rows * wide, -1)
    mine, theirs = meta[2 * CAP], cols_inner[0, 0]
    bits = 0
    for i in range(rows):
        for s in range(slots):
            near = cols_inner[i, s] - theirs
            far = cols_inner[i, s] - mine
            far = jnp.where((far >= 0) & (far < rows), far, rows)
            bits = bits | lax.shift_left(1, far)
            slots_of[i * wide + jnp.where((near >= 0) & (near < rows), near, rows + far)] = s
    rank(bits, rows, order, 0)
    arrive = []
    for r in range(CAP):
        row = meta[CAP + r]
        span = pl.ds(r * block, block)
        for c in range(CAP):
            place = pl.ds(c * block, block)
            slot = slots_of[row * wide + meta[CAP + c]]
            arrive.append(copy_in(x_inner.at[row, jnp.maximum(slot, 0)], got_own.at[span, place], sem_got))
            slot = slots_of[row * wide + rows + order[c]]
            far_slot = jnp.maximum(slot, 0)
            arrive.append(copy_in(x_inner.at[row, far_slot], got_far.at[span, place], sem_got))
    base_near[...] = (twice * outer[...].astype(jnp.float32)
                      + jnp.dot(left_signed, outer[...], preferred_element_type=jnp.float32))
    square[...] = twice * left.astype(jnp.float32) + jnp.dot(left_signed, left, preferred_element_type=jnp.float32)
    for r in range(CAP):
        for c in range(CAP):
            value = outer[pl.ds(pl.multiple_of(asked[c] * block, block), block), pl.ds(r * block, block)]
            weight = sign * kept(table[asked[c] * across + asked[c]])
            turned[pl.ds(r * block, block), pl.ds(c * block, block)] = (value * weight.astype(value.dtype)).T
    for copy in arrive:
        copy.wait()
    for r in range(CAP):
        for c in range(CAP):
            @pl.when(slots_of[meta[CAP + r] * wide + rows + order[c]] < 0)
            def _():
                got_far[pl.ds(r * block, block), pl.ds(c * block, block)] = jnp.zeros((block, block), got_far.dtype)
    part = jnp.dot(inner_signed, got_far[...], preferred_element_type=jnp.float32)
    for c in range(CAP):
        place = pl.ds(pl.multiple_of(order[c] * block, block), block)
        square[:, place] = square[:, place] + part[:, c * block:(c + 1) * block]
    for c in range(CAP):
        place = pl.ds(pl.multiple_of(asked[c] * block, block), block)
        base_far[:, pl.ds(c * block, block)] = square[:, place]
    total = jnp.zeros((block, block), jnp.float32)
    for i in range(rows):
        span = pl.ds(i * block, block)
        total = total + kept(table[i * across + i]) * square[span, span]
    trace[0] = diagonal(total)
    side[...] = twice * inner[...].astype(jnp.float32) + jnp.dot(
        jnp.concatenate([left_signed, inner_signed], axis=1), jnp.concatenate([inner[...], got_own[...]], axis=0),
        preferred_element_type=jnp.float32)
    waits = []
    for i in range(rows):
        span = pl.ds(i * block, block)
        for e in range(rows - CAP):
            k = asked[CAP + e]
            code = table[i * across + k]
            value = square[span, pl.ds(pl.multiple_of(k * block, block), block)]
            stage[i, CAP + e] = (kept(code) * value).astype(stage.dtype)
            waits.append(give(stage.at[i, CAP + e], out, i, code, sem))
        for c in range(CAP):
            code = table[i * across + rows + CAP + c]
            stage[i, c] = (kept(code) * side[span, pl.ds(c * block, block)]).astype(stage.dtype)
            waits.append(give(stage.at[i, c], out, i, code, sem))
    for wait in waits:
        wait()


def trace_kernel(rows, turned, far, trace_own, trace):
    tall, block = turned.shape[0], turned.shape[0] // CAP
    part = far[...].astype(jnp.float32) * turned[...].astype(jnp.float32)
    value = trace_own[0] + jnp.sum(jnp.sum(part.reshape(tall // 8, 8, tall), axis=0))
    trace[...] = jnp.full(trace.shape, value * (1.0 / total_count(rows, block)), jnp.float32)


def total_count(rows, block):
    return rows * block * lax.axis_size(RING)


def finish_half(near, rows, table, asked, outer, base, got, out, stage, sem):
    block = outer.shape[0] // rows
    across = rows + 2 * CAP
    right = got[...] * jnp.where(table[rows * across] == 1, 1.0, -1.0).astype(got.dtype)
    waits = []
    chunk = rows // 2
    for first in range(0, rows, chunk):
        tall = pl.ds(first * block, chunk * block)
        value = base[tall, :] + jnp.dot(outer[tall, :], right, preferred_element_type=jnp.float32)
        codes = {}
        for i in range(first, first + chunk):
            low = (i - first) * block
            for c in range(CAP):
                code = table[i * across + (rows + c if near else asked[c])]
                codes[i, c] = code
                stage[i, c] = (kept(code) * value[low:low + block, c * block:(c + 1) * block]).astype(stage.dtype)
        for (i, c), code in codes.items():
            waits.append(give(stage.at[i, c], out, i, code, sem))
    for wait in waits:
        wait()


def far_kernel(rows, table, asked, outer, base, far, _, out, *scratch):
    finish_half(False, rows, table, asked, outer, base, far, out, *scratch)


def last_kernel(rows, table, asked, outer, base, near, _, out, *scratch):
    finish_half(True, rows, table, asked, outer, base, near, out, *scratch)


def body(x, cols, keep, flag):
    rows, slots, block = x.shape[0], x.shape[1], x.shape[2]
    n = lax.axis_size(RING)
    total_rows = rows * n
    bf16, f32, i32 = x.dtype, jnp.float32, jnp.int32
    wide, narrow, across = rows * block, CAP * block, rows + 2 * CAP
    dma = pltpu.SemaphoreType.DMA

    def ints(*shape):
        return pltpu.SMEM(shape, i32)

    def call(kernel, outs, in_specs, scratch, mib, aliases=None, first=None):
        def run(*refs):
            kernel(*(() if first is None else (first,)), *refs)
        return pl.pallas_call(
            run, out_shape=[(pltpu.HBM if len(o) > 3 else jax.ShapeDtypeStruct)(*o[:2]) for o in outs], in_specs=in_specs,
            out_specs=[o[2] for o in outs], scratch_shapes=scratch, name=kernel.__name__,
            input_output_aliases=aliases or {},
            cost_estimate=pl.CostEstimate(flops=1, bytes_accessed=1, transcendentals=0),
            compiler_params=pltpu.CompilerParams(vmem_limit_bytes=mib * MIB))

    inside = [(i, i ^ 1) for i in range(n)]
    upward = [(i, (i + 1) % n) for i in range(1, n, 2)]
    outside = upward + [(b, a) for a, b in upward]
    hbm = functools.partial(pltpu.with_memory_space_constraint, memory_space=pltpu.HBM)
    barrier = lax.optimization_barrier

    x_inner = permute(x, inside)
    cols_inner = permute(cols, inside)
    cols_outer = permute(cols, outside)
    own, outer, inner, table, meta = call(
        spread_kernel,
        [((wide, wide), bf16, VMEM), ((wide, narrow), bf16, VMEM), ((wide, narrow), bf16, VMEM),
         ((rows * across + 1,), i32, SMEM), ((2 * CAP + 2,), i32, SMEM)],
        [HBM] * 2 + [SMEM, HBM], [ints(rows, slots), ints(rows, slots), pltpu.VMEM(x.shape, bf16), ints(rows * 3 * rows),
                    ints(2 * (CAP + 1)), dma((2 + rows,))], 16, first=total_rows)(hbm(cols), hbm(keep), flag, hbm(x))
    far_out, near_out, asked = call(
        pack_kernel,
        [((narrow, narrow), bf16, VMEM), ((narrow, narrow), bf16, VMEM), ((CAP + rows - CAP + 1,), i32, SMEM)],
        [SMEM] * 2 + [VMEM] * 2, [ints(CAP + 1)], 16,
    )(meta, cols_outer, own, outer)
    far = permute(far_out, outside)
    out, base_far, base_near, turned, trace_own = call(
        own_kernel,
        [(x.shape, bf16, HBM), ((wide, narrow), f32, VMEM), ((wide, narrow), f32, VMEM),
         ((narrow, narrow), bf16, VMEM), ((1,), f32, SMEM)],
        [SMEM] * 4 + [VMEM] * 3 + [HBM],
        [pltpu.VMEM((narrow, narrow), bf16), pltpu.VMEM((narrow, narrow), bf16), pltpu.VMEM((wide, wide), f32),
         pltpu.VMEM((wide, narrow), f32), pltpu.VMEM((rows, rows, block, block), bf16), ints(rows * (2 * rows + 1)),
         ints(CAP + 1), dma, dma], 24)(table, meta, asked, cols_inner, own, outer, inner, x_inner)
    partial, = call(
        trace_kernel, [((8, block), f32, VMEM)], [VMEM, VMEM, SMEM], [], 12, first=rows)(turned, far, trace_own)
    near_out, partial = barrier((near_out, partial))
    near = permute(near_out, outside)
    half_scratch = [pltpu.VMEM((rows, CAP, block, block), bf16), dma]

    def half(kernel, base, got, out):
        result, = call(
            kernel, [(x.shape, bf16, HBM)], [SMEM] * 2 + [VMEM] * 3 + [HBM], half_scratch, 16, {5: 0}, first=rows,
        )(table, asked, outer, base, got, out)
        return result

    steps = ring_steps()
    if steps is None:
        total = lax.psum(partial, RING)
        return half(last_kernel, base_near, near, half(far_kernel, base_far, far, out)), total[0, :1]
    partial = partial + partner(partial, steps[0])
    out, partial = barrier((out, partial))
    out = half(far_kernel, base_far, far, out)
    out, partial = barrier((out, partial))
    for step in steps[1:-1]:
        partial = partial + partner(partial, step)
    ready, partial = barrier((out, partial))
    out = half(last_kernel, base_near, near, ready)
    other, out = barrier((partner(partial, steps[-1] | 1), out))
    return out, (partial + other)[0, :1]


def solution(mesh):
    placed = (
        P(("groups", "row", "col"), None, None, None),
        P(("groups", "row", "col"), None),
        P(("groups", "row", "col"), None),
        P("groups"),
    )
    return jax.shard_map(
        body,
        mesh=mesh,
        in_specs=placed,
        out_specs=(P(("groups", "row", "col"), None, None, None), P("groups")),
        check_vma=False,
    )
```
